32 devices in a mesh: groups: 2 (over x), sector: 16 (over z, y, core).
Axes of the slice: x: 2, y: 2, z: 4, core: 2. Of those that a mesh axis runs over, the one named last changes fastest.
Arguments:
- wave_blocks: bfloat16 [256, 128, 128], P(('groups', 'sector')), parts along dimension 0, may hold values from -6 to 6
- davidson_basis: bfloat16 [4, 256, 128, 128], P(None, ('groups', 'sector')), parts along dimension 1
- left_env: bfloat16 [128, 128, 16, 128], P(('groups', 'sector')), parts along dimension 0, may hold values from -0.125 to 0.125
- right_env: bfloat16 [128, 128, 16, 128], P(('groups', 'sector')), parts along dimension 0, may hold values from -0.25 to 0.25
- source_owner: int32 [512, 1], P('groups'), parts along dimension 0, may hold values from 0 to 15; in each aligned block of 16 rows (0 to 15, 16 to 31, ...) at most 2 rows name the same one
- source_slot: int32 [512], P('groups'), parts along dimension 0, may hold values from 0 to 7
- target_owner: int32 [512, 1], P('groups'), parts along dimension 0, may hold values from 0 to 15; in each aligned block of 16 rows (0 to 15, 16 to 31, ...) at most 2 rows name the same one
- target_slot: int32 [512], P('groups'), parts along dimension 0, may hold values from 0 to 7
Outputs:
- applied: bfloat16 [256, 128, 128], P(('groups', 'sector')), parts along dimension 0
- correlations: float32 [8], P('groups'), parts along dimension 0
The draws below stay inside these ranges and needn't reach their ends.
There are 2 independent parts, one for each index of `groups`. The reference program is written for one: setup_inputs(seed, part) draws one part's arguments, and reference() takes and returns one part's arrays. A program takes and returns all parts, laid end to end along the dimension named above; each array names one. Nothing has to cross between parts.
Inputs may be any that keep to these rules, and one draw needn't show every extreme that they name: `source_owner`: among the 16 rows of one task device no owner appears more than 2 times. `target_owner`: among the 16 rows of one task device no owner appears more than 2 times.
All inputs are finite; a program needn't handle non-finite values.
Results may differ from the reference program's by a relative error of at most 0.0062.
Values may be sent and summed in bfloat16 or wider, within the bound.
A program may use at most 64 MiB of HBM per device.

```python
import math
import jax
import jax.numpy as jnp
import numpy as np
from jax import lax

M = 128
TERMS = 16
LEFT_DEV = 4
RIGHT_DEV = 4
REP = 4
BLK_DEV = 8
CAP = 2
NV = 4
BLOCKS = 128
IN_DEV = 16
OUT_DEV = 16
IN_ROWS = 256
OUT_ROWS = 256
ENVS_L = 64
ENVS_R = 64
N_SECTOR = 16


def draw_davidson_basis(key, part):
    key = jax.random.fold_in(key, 11)
    blocks_axis = jnp.arange(BLOCKS, dtype=jnp.float32)
    ramp = 1.0 + 2.0 * blocks_axis / max(BLOCKS - 1, 1)
    scale = ramp[None, :, None, None] / math.sqrt(BLOCKS * M * M)
    values = jnp.clip(jax.random.normal(key, (NV, BLOCKS, M, M), jnp.float32), -4.0, 4.0)
    return (values * scale).astype(jnp.bfloat16)


def with_ends(entries, key, least, high):
    longest = entries.shape.index(max(entries.shape))
    spots = []
    for shift in (0, 1):
        where = [jax.random.randint(jax.random.fold_in(key, axis), (), 0, length) for axis, length in enumerate(entries.shape)]
        where[longest] = (where[longest] + shift) % entries.shape[longest]
        spots.append(tuple(where))
    return entries.at[spots[0]].set(least).at[spots[1]].set(high)


def block_scale(own_key, extent, cuts, low, top_value):
    gain, own = 1.0, jax.random.fold_in(own_key, 6)
    for axis_at, parts in cuts:
        steps = jnp.exp(jax.random.uniform(jax.random.fold_in(own, axis_at), (parts,), jnp.float32, low / len(cuts), top_value / len(cuts)))
        gain = gain * jnp.repeat(steps, extent[axis_at] // parts).reshape([-1 if axis == axis_at else 1 for axis in range(len(extent))])
    return gain


def routed_block(own_key, own, number, rows, amount, top, most, slope):
    order = jax.random.permutation(own_key, amount)
    packed, common = load_shares(amount, rows * top, most, slope, True), load_shares(amount, rows * top, most, slope, False)
    places = jnp.arange(amount)

    def named(sizes, rotation):
        used = int((sizes > 0).sum())
        fixed = max(1, used // 4)
        passed = fixed + (places - fixed + rotation * (used - fixed)) % max(1, amount - fixed)
        return jnp.zeros((amount,), jnp.int32).at[order[jnp.where(places < fixed, places, passed)]].set(jnp.asarray(sizes, jnp.int32))

    sizes = jnp.where(number % 4 == 0, named(packed, number // 4), named(common, number - number // 4 - 1))
    mixed = jax.random.permutation(jax.random.fold_in(own, 3), amount)
    donor, sink = mixed[0:amount // 2 * 2:2], mixed[1:amount // 2 * 2:2]
    slack = jnp.minimum(sizes[donor] - 1, most - sizes[sink]) // 2
    slack = jnp.where((donor == order[0]) | (sink == order[0]) | (sizes[sink] == 0), 0, jnp.maximum(slack, 0))
    passed = jax.random.randint(jax.random.fold_in(own, 4), (amount // 2,), 0, 1 << 20) % (slack + 1)
    sizes = sizes.at[donor].add(-passed).at[sink].add(passed)
    items = jnp.searchsorted(jnp.cumsum(sizes), jnp.arange(rows * top), side="right").astype(jnp.int32)
    table = items.reshape(top, rows).T
    table = table[jax.random.permutation(jax.random.fold_in(own, 1), rows)]
    rotation = jax.random.randint(jax.random.fold_in(own, 2), (rows, 1), 0, top)
    return jnp.take_along_axis(table, (jnp.arange(top)[None, :] + rotation) % top, axis=1)


def load_shares(number_of, total, bound, lean, full):
    portions = [(1 << 20) // math.isqrt(rank ** lean) + 1 for rank in range(1, number_of + 1)]
    largest = bound if full else min(bound, max(-(-total // number_of), total * portions[0] // sum(portions)))
    least = 1 if total - largest >= number_of - 1 else 0
    counts, surplus = [largest] + [least] * (number_of - 1), total - largest - least * (number_of - 1)
    while surplus > 0:
        free = [i for i in range(1, number_of) if counts[i] < largest] or [i for i in range(1, number_of) if counts[i] < bound]
        pool, remaining = sum([portions[i] for i in free]), surplus
        for i in free:
            extra = min(bound - counts[i], max(1, remaining * portions[i] // pool), surplus)
            counts[i] = counts[i] + extra
            surplus = surplus - extra
    return np.array(counts)


def bell_draw(key, dims, spread, limit, pieces=(), kind=jnp.bfloat16):
    loudness = block_scale(key, dims, pieces, -0.22, 0.18) if pieces else 1.0
    array = jax.random.normal(key, dims, jnp.float32) * spread * loudness
    return jnp.minimum(jnp.maximum(array, -limit), limit).astype(kind)


def setup_inputs(seed: int = 0, part: int = 0) -> dict:
    seeds = jax.random.split(jax.random.key(seed), 9)
    own_keys = jax.random.split(jax.random.fold_in(seeds[8], part), 9)
    wave_blocks = bell_draw(own_keys[0], (BLOCKS, M, M), 1.0, 6.0, ((0, 16),))
    davidson_basis = draw_davidson_basis(jax.random.fold_in(jax.random.fold_in(seeds[8], part), 71), part)
    left_env = bell_draw(own_keys[2], (ENVS_L, M, TERMS, M), (TERMS * M) ** -0.5, 0.125, ((0, 16),))
    right_env = bell_draw(own_keys[3], (ENVS_R, M, TERMS, M), (RIGHT_DEV * M) ** -0.5, 0.25, ((0, 16),))
    source_owner_keys = jax.random.split(jax.random.fold_in(own_keys[4], 1), IN_ROWS // IN_DEV)
    source_owner_turns = jax.random.permutation(jax.random.fold_in(own_keys[4], 3), IN_ROWS // IN_DEV)
    source_owner = jax.vmap(lambda own, number: routed_block(jax.random.fold_in(own_keys[4], 2), own, number, IN_DEV, N_SECTOR, 1, CAP, 2))(source_owner_keys, source_owner_turns).reshape((IN_ROWS, 1))
    source_slot = with_ends(jax.random.randint(own_keys[5], (IN_ROWS,), 0, BLK_DEV), jax.random.fold_in(own_keys[5], 1), 0, BLK_DEV - 1).astype(jnp.int32)
    target_owner_keys = jax.random.split(jax.random.fold_in(own_keys[6], 1), OUT_ROWS // OUT_DEV)
    target_owner_turns = jax.random.permutation(jax.random.fold_in(own_keys[6], 3), OUT_ROWS // OUT_DEV)
    target_owner = jax.vmap(lambda own, number: routed_block(jax.random.fold_in(own_keys[6], 2), own, number, OUT_DEV, N_SECTOR, 1, CAP, 2))(target_owner_keys, target_owner_turns).reshape((OUT_ROWS, 1))
    target_slot = with_ends(jax.random.randint(own_keys[7], (OUT_ROWS,), 0, BLK_DEV), jax.random.fold_in(own_keys[7], 1), 0, BLK_DEV - 1).astype(jnp.int32)
    return {"wave_blocks": wave_blocks, "davidson_basis": davidson_basis, "left_env": left_env, "right_env": right_env, "source_owner": source_owner, "source_slot": source_slot, "target_owner": target_owner, "target_slot": target_slot}


def contract_device(operands):
    inputs, right_part, left_part = operands
    contracted = jnp.einsum("bclr,brws->cwls", inputs.astype(jnp.float32), right_part.astype(jnp.float32)).astype(jnp.bfloat16)
    return jnp.einsum("axwl,cwls->acxs", left_part.astype(jnp.float32), contracted.astype(jnp.float32)).astype(jnp.bfloat16)


def reference(wave_blocks, davidson_basis, left_env, right_env, source_owner, source_slot, target_owner, target_slot):
    sources = (source_owner[:, 0] * BLK_DEV + source_slot).astype(jnp.int32)
    targets = (target_owner[:, 0] * BLK_DEV + target_slot).astype(jnp.int32)
    inputs = wave_blocks[sources].reshape(N_SECTOR, RIGHT_DEV, REP, M, M)
    right_part = right_env.reshape(N_SECTOR, RIGHT_DEV, M, TERMS, M)
    left_part = left_env.reshape(N_SECTOR, LEFT_DEV, M, TERMS, M)
    results = lax.map(contract_device, (inputs, right_part, left_part))
    results = results.reshape(OUT_ROWS, M, M)
    applied = jax.ops.segment_sum(results.astype(jnp.float32), targets, num_segments=BLOCKS).astype(jnp.bfloat16)
    correlations = jnp.einsum("vbxy,bxy->v", davidson_basis.astype(jnp.float32), applied.astype(jnp.float32))
    return applied, correlations
```

```python
import functools

import jax
import jax.numpy as jnp
from jax import lax
from jax.experimental import pallas as pl
from jax.experimental.pallas import tpu as pltpu
from jax.sharding import PartitionSpec as P

CAP = 2
CHUNKS = 2
MESH = pl.DeviceIdType.MESH


def two_hits(owner_ref, base, rows, who, value, default):
    def step(at, found):
        first, second = found
        row = rows - 1 - at
        hit = owner_ref[base + row] == who
        return jnp.where(hit, value(row), first), jnp.where(hit, first, second)

    start = (jnp.int32(default), jnp.int32(default))
    return lax.fori_loop(0, rows, step, start, unroll=16)


def kernel(
    n,
    repeats,
    sown,
    sslot,
    town,
    tslot,
    wave_hbm,
    dav_hbm,
    left_hbm,
    right_hbm,
    applied_ref,
    corr_ref,
    wave,
    dav,
    raw_r,
    raw_l,
    flat_r,
    flat_l,
    in_send0,
    in_send1,
    in_recv0,
    in_recv1,
    operand,
    contracted,
    res0,
    res1,
    out_send0,
    out_send1,
    out_recv0,
    out_recv1,
    acc,
    corr_part,
    corr_send,
    corr_recv,
    landing,
    load_sem,
    right_sem,
    left_sem,
    in_ssem,
    in_rsem,
    out_ssem,
    out_rsem,
    corr_ssem,
    corr_rsem,
):
    me = lax.axis_index("sector")
    rows = sslot.shape[0] // n
    owned, width = wave.shape[0], wave.shape[1]
    envs = right_hbm.shape[0]
    terms = right_hbm.shape[2]
    nv = dav.shape[0]
    part = width // CHUNKS
    in_send, in_recv = (in_send0, in_send1), (in_recv0, in_recv1)
    res = (res0, res1)
    out_send, out_recv = (out_send0, out_send1), (out_recv0, out_recv1)

    def peer(t):
        off = n // 2 + (1 - 2 * (t % 2)) * ((t + 1) // 2)
        return lax.rem(me + off, n)

    def source(t):
        off = n // 2 + (1 - 2 * (t % 2)) * ((t + 1) // 2)
        return lax.rem(me - off + n, n)

    load_wave = pltpu.make_async_copy(wave_hbm, wave, load_sem.at[0])
    load_dav = pltpu.make_async_copy(dav_hbm, dav, load_sem.at[1])

    def load_right(b):
        return pltpu.make_async_copy(right_hbm.at[b], raw_r.at[b], right_sem.at[b])

    def load_left(a):
        return pltpu.make_async_copy(left_hbm.at[a], raw_l.at[a], left_sem.at[a])

    load_wave.start()
    for b in range(envs):
        load_right(b).start()
    for a in range(envs):
        load_left(a).start()
    load_dav.start()

    barrier = pltpu.get_barrier_semaphore()

    @pl.loop(0, n - 1)
    def _(t):
        pl.semaphore_signal(
            barrier, inc=1, device_id={"sector": peer(t)}, device_id_type=MESH
        )

    load_wave.wait()

    def pick(p):
        return two_hits(sown, p * rows, rows, me, lambda row: sslot[p * rows + row], 0)

    own0, own1 = pick(me)
    for k, slot in enumerate((own0, own1)):
        for q in range(CHUNKS):
            in_recv[q][me, k] = wave[slot, q * part : (q + 1) * part, :]

    pl.semaphore_wait(barrier, n - 1)

    def in_copy(q, to, frm):
        return pltpu.make_async_remote_copy(
            src_ref=in_send[q].at[to],
            dst_ref=in_recv[q].at[frm],
            send_sem=in_ssem.at[q, to],
            recv_sem=in_rsem.at[q, frm],
            device_id={"sector": to},
            device_id_type=MESH,
        )

    @pl.loop(0, n - 1)
    def _(t):
        p = peer(t)
        slots = pick(p)
        for k in range(CAP):
            for q in range(CHUNKS):
                in_send[q][p, k] = wave[slots[k], q * part : (q + 1) * part, :]
        in_copy(0, p, me).start()

    @pl.loop(0, n - 1)
    def _(t):
        in_copy(1, peer(t), me).start()

    tile = 16
    for b in range(envs):
        load_right(b).wait()

    @pl.loop(0, envs * width // tile)
    def _(i):
        b = i // (width // tile)
        r = (i % (width // tile)) * tile
        r = pl.multiple_of(r, tile)
        block = jnp.swapaxes(raw_r[b, pl.ds(r, tile)], 0, 1)
        for w in range(terms):
            flat_r[pl.ds(pl.multiple_of(b * width + r, tile), tile), w * width : (w + 1) * width] = block[w]

    for a in range(envs):
        load_left(a).wait()

    @pl.loop(0, envs * width // tile)
    def _(i):
        a = i // (width // tile)
        x = (i % (width // tile)) * tile
        x = pl.multiple_of(x, tile)
        q = x // part
        block = jnp.swapaxes(raw_l[a, pl.ds(x, tile)], 0, 1)
        at = pl.multiple_of(q * envs * part + a * part + x % part, tile)
        for w in range(terms):
            flat_l[pl.ds(at, tile), w * width : (w + 1) * width] = block[w]

    @pl.loop(0, n)
    def _(j):
        hits = two_hits(town, j * rows, rows, me, lambda row: tslot[j * rows + row], -1)
        for k in range(CAP):
            landing[j * CAP + k] = hits[k]

    acc[...] = jnp.zeros_like(acc)
    load_dav.wait()

    for q in range(CHUNKS):

        @pl.loop(0, n - 1)
        def _(t):
            in_copy(q, source(t), source(t)).wait_recv()

        @pl.loop(0, rows)
        def _(i):
            owner = sown[me * rows + i]

            def count(h, seen):
                same = (sown[me * rows + h] == owner) & (h < i)
                return seen + same.astype(jnp.int32)

            rank = lax.fori_loop(0, rows, count, jnp.int32(0), unroll=16)
            b = i // repeats
            c = i % repeats
            operand[
                pl.ds(pl.multiple_of(c * part, part), part),
                pl.ds(pl.multiple_of(b * width, width), width),
            ] = in_recv[q][owner, jnp.minimum(rank, CAP - 1)]

        @pl.loop(0, terms // 2)
        def _(pair):
            cols = pl.ds(pl.multiple_of(pair * 2 * width, 2 * width), 2 * width)
            out = jnp.dot(
                operand[...], flat_r[:, cols], preferred_element_type=jnp.float32
            ).astype(jnp.bfloat16)
            for c in range(repeats):
                for h in range(2):
                    at = pl.multiple_of((pair * 2 + h) * width + q * part, part)
                    contracted[pl.ds(at, part), c * width : (c + 1) * width] = out[
                        c * part : (c + 1) * part, h * width : (h + 1) * width
                    ]

    def out_copy(q, to, frm):
        return pltpu.make_async_remote_copy(
            src_ref=out_send[q].at[to],
            dst_ref=out_recv[q].at[frm],
            send_sem=out_ssem.at[q, to],
            recv_sem=out_rsem.at[q, frm],
            device_id={"sector": to},
            device_id_type=MESH,
        )

    for q in range(CHUNKS):
        lhs_rows = slice(q * envs * part, (q + 1) * envs * part)

        @pl.loop(0, repeats // 2)
        def _(pair):
            cols = pl.ds(pl.multiple_of(pair * 2 * width, 2 * width), 2 * width)
            out = jnp.dot(
                flat_l[lhs_rows, :], contracted[:, cols], preferred_element_type=jnp.float32
            ).astype(jnp.bfloat16)
            for a in range(envs):
                for h in range(2):
                    res[q][a * repeats + pair * 2 + h] = out[
                        a * part : (a + 1) * part, h * width : (h + 1) * width
                    ]

        def choose(p):
            return two_hits(town, me * rows, rows, p, lambda row: row, 0)

        @pl.loop(0, n - 1)
        def _(t):
            p = peer(t)
            picked = choose(p)
            for k in range(CAP):
                out_send[q][p, k] = res[q][picked[k]]
            out_copy(q, p, me).start()

        picked = choose(me)
        for k in range(CAP):
            out_recv[q][me, k] = res[q][picked[k]]

    def add(q, j):
        values = [out_recv[q][j, k].astype(jnp.float32) for k in range(CAP)]
        lands = [landing[j * CAP + k] for k in range(CAP)]
        for d in range(owned):
            total = acc[q, d]
            for k in range(CAP):
                total = total + jnp.where(lands[k] == d, 1.0, 0.0) * values[k]
            acc[q, d] = total

    partial = [jnp.zeros((8, width), jnp.float32) for _ in range(nv)]
    for q in range(CHUNKS):
        add(q, me)

        @pl.loop(0, n - 1)
        def _(t):
            j = source(t)
            out_copy(q, j, j).wait_recv()
            add(q, j)

        for d in range(owned):
            block = acc[q, d].astype(jnp.bfloat16)
            applied_ref[d, q * part : (q + 1) * part, :] = block
            block = block.astype(jnp.float32)
            for v in range(nv):
                prod = dav[v, d, q * part : (q + 1) * part, :].astype(jnp.float32) * block
                partial[v] = partial[v] + jnp.sum(prod.reshape(part // 8, 8, width), axis=0)

    for v in range(nv):
        corr_send[v : v + 1, :] = jnp.sum(partial[v], axis=0, keepdims=True)
    if nv < corr_send.shape[0]:
        corr_send[nv:, :] = jnp.zeros((corr_send.shape[0] - nv, width), jnp.float32)

    def corr_copy(to, frm):
        return pltpu.make_async_remote_copy(
            src_ref=corr_send,
            dst_ref=corr_recv.at[frm],
            send_sem=corr_ssem.at[to],
            recv_sem=corr_rsem.at[frm],
            device_id={"sector": to},
            device_id_type=MESH,
        )

    @pl.loop(0, n - 1)
    def _(t):
        corr_copy(peer(t), me).start()

    corr_recv[me] = corr_send[...]

    @pl.loop(0, n - 1)
    def _(t):
        p = peer(t)
        for q in range(CHUNKS):
            in_copy(q, p, me).wait_send()
            out_copy(q, p, me).wait_send()

    @pl.loop(0, n - 1)
    def _(t):
        corr_copy(source(t), source(t)).wait_recv()

    total = jnp.sum(corr_recv[...], axis=0)
    for v in range(nv):
        corr_ref[v] = jnp.sum(total[v : v + 1, :])

    @pl.loop(0, n - 1)
    def _(t):
        corr_copy(peer(t), me).wait_send()


def shards(
    wave_blocks,
    davidson_basis,
    left_env,
    right_env,
    source_owner,
    source_slot,
    target_owner,
    target_slot,
):
    n = lax.axis_size("sector")
    owned, width = wave_blocks.shape[0], wave_blocks.shape[1]
    envs, terms = right_env.shape[0], right_env.shape[2]
    rows = source_slot.shape[0] // n
    repeats = rows // envs
    nv = davidson_basis.shape[0]
    part = width // CHUNKS
    corr_rows = -(-nv // 8) * 8
    bf16 = jnp.bfloat16
    smem = pl.BlockSpec(memory_space=pltpu.SMEM)
    vmem = pl.BlockSpec(memory_space=pltpu.VMEM)
    hbm = pl.BlockSpec(memory_space=pl.ANY)
    dma = pltpu.SemaphoreType.DMA
    flops = 4 * rows * terms * width**3
    return pl.pallas_call(
        functools.partial(kernel, n, repeats),
        out_shape=(
            jax.ShapeDtypeStruct((owned, width, width), bf16),
            jax.ShapeDtypeStruct((nv,), jnp.float32),
        ),
        in_specs=[smem] * 4 + [hbm] * 4,
        out_specs=(vmem, smem),
        scratch_shapes=[
            pltpu.VMEM((owned, width, width), bf16),
            pltpu.VMEM((nv, owned, width, width), bf16),
            pltpu.VMEM((envs, width, terms, width), bf16),
            pltpu.VMEM((envs, width, terms, width), bf16),
            pltpu.VMEM((envs * width, terms * width), bf16),
            pltpu.VMEM((envs * width, terms * width), bf16),
            pltpu.VMEM((n, CAP, part, width), bf16),
            pltpu.VMEM((n, CAP, part, width), bf16),
            pltpu.VMEM((n, CAP, part, width), bf16),
            pltpu.VMEM((n, CAP, part, width), bf16),
            pltpu.VMEM((repeats * part, envs * width), bf16),
            pltpu.VMEM((terms * width, repeats * width), bf16),
            pltpu.VMEM((rows, part, width), bf16),
            pltpu.VMEM((rows, part, width), bf16),
            pltpu.VMEM((n, CAP, part, width), bf16),
            pltpu.VMEM((n, CAP, part, width), bf16),
            pltpu.VMEM((n, CAP, part, width), bf16),
            pltpu.VMEM((n, CAP, part, width), bf16),
            pltpu.VMEM((CHUNKS, owned, part, width), jnp.float32),
            pltpu.VMEM((nv, 8, width), jnp.float32),
            pltpu.VMEM((corr_rows, width), jnp.float32),
            pltpu.VMEM((n, corr_rows, width), jnp.float32),
            pltpu.SMEM((n * CAP,), jnp.int32),
            dma((2,)),
            dma((envs,)),
            dma((envs,)),
            dma((CHUNKS, n)),
            dma((CHUNKS, n)),
            dma((CHUNKS, n)),
            dma((CHUNKS, n)),
            dma((n,)),
            dma((n,)),
        ],
        compiler_params=pltpu.CompilerParams(
            collective_id=0, has_side_effects=True, vmem_limit_bytes=60 * 2**20
        ),
        cost_estimate=pl.CostEstimate(
            flops=flops, bytes_accessed=10 * 2**20, transcendentals=0
        ),
    )(
        source_owner.reshape(-1),
        source_slot,
        target_owner.reshape(-1),
        target_slot,
        wave_blocks,
        davidson_basis,
        left_env,
        right_env,
    )


def solution(mesh):
    return jax.shard_map(
        shards,
        mesh=mesh,
        in_specs=(
            P(("groups", "sector"), None, None),
            P(None, ("groups", "sector"), None, None),
            P(("groups", "sector"), None, None, None),
            P(("groups", "sector"), None, None, None),
            P("groups", None),
            P("groups"),
            P("groups", None),
            P("groups"),
        ),
        out_specs=(P(("groups", "sector"), None, None), P("groups")),
        check_vma=False,
    )
```

```python
import functools

import jax
import jax.numpy as jnp
from jax import lax
from jax.experimental import pallas as pl
from jax.experimental.pallas import tpu as pltpu
from jax.sharding import PartitionSpec as P

CAP = 2
CHUNKS = 2
LINE = 4
MESH = pl.DeviceIdType.MESH


def two_hits(owner_ref, base, rows, who, value, default):
    def step(at, found):
        first, second = found
        row = rows - 1 - at
        hit = owner_ref[base + row] == who
        return jnp.where(hit, value(row), first), jnp.where(hit, first, second)

    start = (jnp.int32(default), jnp.int32(default))
    return lax.fori_loop(0, rows, step, start, unroll=16)


def kernel(
    n,
    repeats,
    sown,
    sslot,
    town,
    tslot,
    wave_hbm,
    dav_hbm,
    left_hbm,
    right_hbm,
    applied_ref,
    corr_ref,
    wave,
    dav,
    raw_r,
    raw_l,
    flat_r,
    flat_l,
    operand,
    contracted,
    acc,
    corr_send,
    corr_recv,
    corr_col,
    corr_lin,
    take,
    rank_of,
    chosen,
    landing,
    load_sem,
    right_sem,
    left_sem,
    raw_ssem,
    raw_rsem,
    col_ssem,
    col_rsem,
    ocol_ssem,
    ocol_rsem,
    line_ssem,
    line_rsem,
    corr_ssem,
    corr_rsem,
    corz_ssem,
    corz_rsem,
    *parts,
):
    me = lax.axis_index("sector")
    side = n // LINE
    z, r = me // side, me % side
    rows = sslot.shape[0] // n
    owned, width = wave.shape[0], wave.shape[1]
    envs = right_hbm.shape[0]
    terms = right_hbm.shape[2]
    nv = dav.shape[0]
    part = width // CHUNKS
    hops = LINE - 1
    grouped = [parts[at * CHUNKS : (at + 1) * CHUNKS] for at in range(len(parts) // CHUNKS)]
    relay = [[grouped[d * hops + k] for k in range(hops)] for d in range(2)]
    col_send, in_recv, res, ocol_send, ocol_recv, line_send, line_recv = grouped[2 * hops :]
    step = (1, -1)

    def has(d, k):
        return z >= k if d == 0 else z + k < LINE

    def next_of(d):
        return jnp.clip(z + step[d], 0, LINE - 1) * side + r

    load_wave = pltpu.make_async_copy(wave_hbm, wave, load_sem.at[0])
    load_dav = pltpu.make_async_copy(dav_hbm, dav, load_sem.at[1])

    def load_right(b):
        return pltpu.make_async_copy(right_hbm.at[b], raw_r.at[b], right_sem.at[b])

    def load_left(a):
        return pltpu.make_async_copy(left_hbm.at[a], raw_l.at[a], left_sem.at[a])

    barrier = pltpu.get_barrier_semaphore()

    for o in range(1, LINE):
        pl.semaphore_signal(
            barrier,
            inc=1,
            device_id={"sector": lax.rem(z + o, LINE) * side + r},
            device_id_type=MESH,
        )

    @pl.loop(1, side)
    def _(o):
        pl.semaphore_signal(
            barrier,
            inc=1,
            device_id={"sector": z * side + lax.rem(r + o, side)},
            device_id_type=MESH,
        )

    load_wave.start()
    for b in range(envs):
        load_right(b).start()
    for a in range(envs):
        load_left(a).start()
    load_dav.start()

    @pl.loop(0, n)
    def _(at):
        s, to = at // side, at % side
        base = (z * side + to) * rows
        hits = two_hits(sown, base, rows, s * side + r, lambda row: sslot[base + row], 0)
        for k in range(CAP):
            take[at * CAP + k] = hits[k]

    load_wave.wait()

    def raw_copy(d, k, q):
        src = wave.at[:, q * part : (q + 1) * part, :] if k == 0 else relay[d][k - 1][q]
        return pltpu.make_async_remote_copy(
            src_ref=src,
            dst_ref=relay[d][k][q],
            send_sem=raw_ssem.at[d, k, q],
            recv_sem=raw_rsem.at[d, k, q],
            device_id={"sector": next_of(d)},
            device_id_type=MESH,
        )

    def col_copy(q, s, to, frm):
        return pltpu.make_async_remote_copy(
            src_ref=col_send[q].at[s, to],
            dst_ref=in_recv[q].at[s * side + frm],
            send_sem=col_ssem.at[q, s, to],
            recv_sem=col_rsem.at[q, s, frm],
            device_id={"sector": z * side + to},
            device_id_type=MESH,
        )

    def hand_out(q, s, load):
        @pl.loop(1, side)
        def _(o):
            to = lax.rem(r + o, side)
            for k in range(CAP):
                col_send[q][s, to, k] = load(take[(s * side + to) * CAP + k])
            col_copy(q, s, to, r).start()

        for k in range(CAP):
            in_recv[q][s * side + r, k] = load(take[(s * side + r) * CAP + k])

    pl.semaphore_wait(barrier, LINE - 1 + side - 1)

    for q in range(CHUNKS):
        for d in range(2):
            ahead = z < LINE - 1 if d == 0 else z > 0

            @pl.when(ahead)
            def _():
                raw_copy(d, 0, q).start()

    for q in range(CHUNKS):
        hand_out(q, z, lambda slot: wave[slot, q * part : (q + 1) * part, :])

    tile = 16
    per_env = width // tile

    def flatten_right(b):
        load_right(b).wait()

        @pl.loop(0, per_env)
        def _(i):
            at = pl.multiple_of(i * tile, tile)
            block = jnp.swapaxes(raw_r[b, pl.ds(at, tile)], 0, 1)
            to = pl.multiple_of(b * width + at, tile)
            for w in range(terms):
                flat_r[pl.ds(to, tile), w * width : (w + 1) * width] = block[w]

    def flatten_left(a):
        load_left(a).wait()

        @pl.loop(0, per_env)
        def _(i):
            x = pl.multiple_of(i * tile, tile)
            block = jnp.swapaxes(raw_l[a, pl.ds(x, tile)], 0, 1)
            to = pl.multiple_of((x // part) * envs * part + a * part + x % part, tile)
            for w in range(terms):
                flat_l[pl.ds(to, tile), w * width : (w + 1) * width] = block[w]

    def ranks():
        @pl.loop(0, rows)
        def _(i):
            owner = sown[me * rows + i]

            def count(h, seen):
                same = (sown[me * rows + h] == owner) & (h < i)
                return seen + same.astype(jnp.int32)

            rank = lax.fori_loop(0, rows, count, jnp.int32(0), unroll=16)
            rank_of[i] = owner * CAP + jnp.minimum(rank, CAP - 1)

    def result_tables():
        @pl.loop(0, n)
        def _(p):
            hits = two_hits(town, me * rows, rows, p, lambda row: row, 0)
            for k in range(CAP):
                chosen[p * CAP + k] = hits[k]

        @pl.loop(0, n)
        def _(at):
            s, frm = at // side, at % side
            base = (z * side + frm) * rows
            hits = two_hits(town, base, rows, s * side + r, lambda row: tslot[base + row], -1)
            for k in range(CAP):
                landing[at * CAP + k] = hits[k]

    chores = [functools.partial(flatten_right, b) for b in range(envs)]
    chores += [functools.partial(flatten_left, a) for a in range(envs)]
    chores += [ranks, result_tables]
    stops = hops * CHUNKS
    stop = 0
    for k in range(hops):
        for q in range(CHUNKS):
            for chore in chores[stop * len(chores) // stops : (stop + 1) * len(chores) // stops]:
                chore()
            stop += 1
            for d in range(2):

                @pl.when(has(d, k + 1))
                def _():
                    raw_copy(d, k, q).wait_recv()
                    if k + 1 < hops:
                        ahead = z < LINE - 1 if d == 0 else z > 0

                        @pl.when(ahead)
                        def _():
                            raw_copy(d, k + 1, q).start()

            for d in range(2):

                @pl.when(has(d, k + 1))
                def _():
                    hand_out(q, z - step[d] * (k + 1), lambda slot: relay[d][k][q][slot])

    for q in range(CHUNKS):

        @pl.loop(0, LINE * (side - 1))
        def _(t):
            frm = lax.rem(r + 1 + t % (side - 1), side)
            col_copy(q, t // (side - 1), frm, frm).wait_recv()

        @pl.loop(0, rows)
        def _(i):
            b = i // repeats
            c = i % repeats
            at = rank_of[i]
            operand[
                pl.ds(pl.multiple_of(c * part, part), part),
                pl.ds(pl.multiple_of(b * width, width), width),
            ] = in_recv[q][at // CAP, at % CAP]

        @pl.loop(0, terms // 2)
        def _(pair):
            cols = pl.ds(pl.multiple_of(pair * 2 * width, 2 * width), 2 * width)
            out = jnp.dot(
                operand[...], flat_r[:, cols], preferred_element_type=jnp.float32
            ).astype(jnp.bfloat16)
            for c in range(repeats):
                for h in range(2):
                    at = pl.multiple_of((pair * 2 + h) * width + q * part, part)
                    contracted[pl.ds(at, part), c * width : (c + 1) * width] = out[
                        c * part : (c + 1) * part, h * width : (h + 1) * width
                    ]

    def ocol_copy(q, s, to, frm):
        return pltpu.make_async_remote_copy(
            src_ref=ocol_send[q].at[s, to],
            dst_ref=ocol_recv[q].at[s, frm],
            send_sem=ocol_ssem.at[q, s, to],
            recv_sem=ocol_rsem.at[q, s, frm],
            device_id={"sector": z * side + to},
            device_id_type=MESH,
        )

    def target(t):
        return jnp.where(z < LINE // 2, LINE - 1 - t, t)

    for q in range(CHUNKS):
        lhs_rows = slice(q * envs * part, (q + 1) * envs * part)

        @pl.loop(0, repeats // 2)
        def _(pair):
            cols = pl.ds(pl.multiple_of(pair * 2 * width, 2 * width), 2 * width)
            out = jnp.dot(
                flat_l[lhs_rows, :], contracted[:, cols], preferred_element_type=jnp.float32
            ).astype(jnp.bfloat16)
            for a in range(envs):
                for h in range(2):
                    res[q][a * repeats + pair * 2 + h] = out[
                        a * part : (a + 1) * part, h * width : (h + 1) * width
                    ]

        @pl.loop(0, LINE)
        def _(t):
            s = target(t)

            @pl.loop(1, side)
            def _(o):
                to = lax.rem(r + o, side)
                for k in range(CAP):
                    ocol_send[q][s, to, k] = res[q][chosen[(s * side + to) * CAP + k]]
                ocol_copy(q, s, to, r).start()

            for k in range(CAP):
                ocol_recv[q][s, r, k] = res[q][chosen[(s * side + r) * CAP + k]]

    def column_sum(q, s):
        @pl.loop(1, side)
        def _(o):
            frm = lax.rem(r + o, side)
            ocol_copy(q, s, frm, frm).wait_recv()

        @pl.loop(0, part // tile)
        def _(i):
            at = pl.ds(pl.multiple_of(i * tile, tile), tile)

            def add(frm, totals):
                totals = list(totals)
                for k in range(CAP):
                    value = ocol_recv[q][s, frm, k, at].astype(jnp.float32)
                    land = landing[(s * side + frm) * CAP + k]
                    for b in range(owned):
                        totals[b] = totals[b] + jnp.where(land == b, 1.0, 0.0) * value
                return tuple(totals)

            zero = tuple(jnp.zeros((tile, width), jnp.float32) for _ in range(owned))
            totals = lax.fori_loop(0, side, add, zero, unroll=4)
            for b in range(owned):
                acc[b, at] = totals[b]

    def line_copy(d, k, q):
        return pltpu.make_async_remote_copy(
            src_ref=line_send[q].at[d, k],
            dst_ref=line_recv[q].at[d, k],
            send_sem=line_ssem.at[d, k, q],
            recv_sem=line_rsem.at[d, k, q],
            device_id={"sector": next_of(d)},
            device_id_type=MESH,
        )

    def add_line(d, k, q):
        line_copy(d, k, q).wait_recv()

        @pl.loop(0, owned)
        def _(b):
            acc[b] = acc[b] + line_recv[q][d, k, b].astype(jnp.float32)

    for k in reversed(range(hops)):
        for q in range(CHUNKS):
            for d in range(2):
                exists = z + k + 1 < LINE if d == 0 else z >= k + 1

                @pl.when(exists)
                def _():
                    column_sum(q, z + step[d] * (k + 1))
                    if k + 1 < hops:

                        @pl.when(has(d, 1))
                        def _():
                            add_line(d, k + 1, q)

                    @pl.loop(0, owned)
                    def _(b):
                        line_send[q][d, k, b] = acc[b].astype(jnp.bfloat16)

                    line_copy(d, k, q).start()

    load_dav.wait()
    partial = [jnp.zeros((8, width), jnp.float32) for _ in range(nv)]
    for q in range(CHUNKS):
        column_sum(q, z)
        for d in range(2):

            @pl.when(has(d, 1))
            def _():
                add_line(d, 0, q)

        for b in range(owned):
            block = acc[b].astype(jnp.bfloat16)
            applied_ref[b, q * part : (q + 1) * part, :] = block
            block = block.astype(jnp.float32)
            for v in range(nv):
                prod = dav[v, b, q * part : (q + 1) * part, :].astype(jnp.float32) * block
                partial[v] = partial[v] + jnp.sum(prod.reshape(part // 8, 8, width), axis=0)

    for v in range(nv):
        corr_send[v : v + 1, :] = jnp.sum(partial[v], axis=0, keepdims=True)
    if nv < corr_send.shape[0]:
        corr_send[nv:, :] = jnp.zeros((corr_send.shape[0] - nv, width), jnp.float32)

    def corr_copy(to, frm):
        return pltpu.make_async_remote_copy(
            src_ref=corr_send,
            dst_ref=corr_recv.at[frm],
            send_sem=corr_ssem.at[to],
            recv_sem=corr_rsem.at[frm],
            device_id={"sector": z * side + to},
            device_id_type=MESH,
        )

    def corz_copy(to, frm):
        return pltpu.make_async_remote_copy(
            src_ref=corr_col,
            dst_ref=corr_lin.at[frm],
            send_sem=corz_ssem.at[to],
            recv_sem=corz_rsem.at[frm],
            device_id={"sector": to * side + r},
            device_id_type=MESH,
        )

    @pl.loop(1, side)
    def _(o):
        corr_copy(lax.rem(r + o, side), r).start()

    corr_recv[r] = corr_send[...]

    for q in range(CHUNKS):

        @pl.loop(0, LINE * (side - 1))
        def _(t):
            to = lax.rem(r + 1 + t % (side - 1), side)
            col_copy(q, t // (side - 1), to, r).wait_send()
            ocol_copy(q, t // (side - 1), to, r).wait_send()

        for d in range(2):
            for k in range(hops):
                ahead = z < LINE - 1 if d == 0 else z > 0

                @pl.when(ahead & has(d, k))
                def _():
                    raw_copy(d, k, q).wait_send()

                exists = z + k + 1 < LINE if d == 0 else z >= k + 1

                @pl.when(exists)
                def _():
                    line_copy(d, k, q).wait_send()

    @pl.loop(1, side)
    def _(o):
        frm = lax.rem(r + o, side)
        corr_copy(frm, frm).wait_recv()

    corr_col[...] = jnp.sum(corr_recv[...], axis=0)
    for o in range(1, LINE):
        corz_copy(lax.rem(z + o, LINE), z).start()
    corr_lin[z] = corr_col[...]

    @pl.loop(1, side)
    def _(o):
        corr_copy(lax.rem(r + o, side), r).wait_send()

    for o in range(1, LINE):
        frm = lax.rem(z + o, LINE)
        corz_copy(frm, frm).wait_recv()

    total = jnp.sum(corr_lin[...], axis=0)
    for v in range(nv):
        corr_ref[v] = jnp.sum(total[v : v + 1, :])

    for o in range(1, LINE):
        corz_copy(lax.rem(z + o, LINE), z).wait_send()


def shards(
    wave_blocks,
    davidson_basis,
    left_env,
    right_env,
    source_owner,
    source_slot,
    target_owner,
    target_slot,
):
    n = lax.axis_size("sector")
    owned, width = wave_blocks.shape[0], wave_blocks.shape[1]
    envs, terms = right_env.shape[0], right_env.shape[2]
    rows = source_slot.shape[0] // n
    repeats = rows // envs
    nv = davidson_basis.shape[0]
    part = width // CHUNKS
    side, hops = n // LINE, LINE - 1
    corr_rows = -(-nv // 8) * 8
    bf16 = jnp.bfloat16
    smem = pl.BlockSpec(memory_space=pltpu.SMEM)
    vmem = pl.BlockSpec(memory_space=pltpu.VMEM)
    hbm = pl.BlockSpec(memory_space=pl.ANY)
    dma = pltpu.SemaphoreType.DMA
    flops = 4 * rows * terms * width**3
    return pl.pallas_call(
        functools.partial(kernel, n, repeats),
        out_shape=(
            jax.ShapeDtypeStruct((owned, width, width), bf16),
            jax.ShapeDtypeStruct((nv,), jnp.float32),
        ),
        in_specs=[smem] * 4 + [hbm] * 4,
        out_specs=(vmem, smem),
        scratch_shapes=[
            pltpu.VMEM((owned, width, width), bf16),
            pltpu.VMEM((nv, owned, width, width), bf16),
            pltpu.VMEM((envs, width, terms, width), bf16),
            pltpu.VMEM((envs, width, terms, width), bf16),
            pltpu.VMEM((envs * width, terms * width), bf16),
            pltpu.VMEM((envs * width, terms * width), bf16),
            pltpu.VMEM((repeats * part, envs * width), bf16),
            pltpu.VMEM((terms * width, repeats * width), bf16),
            pltpu.VMEM((owned, part, width), jnp.float32),
            pltpu.VMEM((corr_rows, width), jnp.float32),
            pltpu.VMEM((side, corr_rows, width), jnp.float32),
            pltpu.VMEM((corr_rows, width), jnp.float32),
            pltpu.VMEM((LINE, corr_rows, width), jnp.float32),
            pltpu.SMEM((n * CAP,), jnp.int32),
            pltpu.SMEM((rows,), jnp.int32),
            pltpu.SMEM((n * CAP,), jnp.int32),
            pltpu.SMEM((n * CAP,), jnp.int32),
            dma((2,)),
            dma((envs,)),
            dma((envs,)),
            dma((2, hops, CHUNKS)),
            dma((2, hops, CHUNKS)),
            dma((CHUNKS, LINE, side)),
            dma((CHUNKS, LINE, side)),
            dma((CHUNKS, LINE, side)),
            dma((CHUNKS, LINE, side)),
            dma((2, hops, CHUNKS)),
            dma((2, hops, CHUNKS)),
            dma((side,)),
            dma((side,)),
            dma((LINE,)),
            dma((LINE,)),
        ]
        + [pltpu.VMEM((owned, part, width), bf16)] * (2 * hops * CHUNKS)
        + [pltpu.VMEM((LINE, side, CAP, part, width), bf16)] * CHUNKS
        + [pltpu.VMEM((n, CAP, part, width), bf16)] * CHUNKS
        + [pltpu.VMEM((rows, part, width), bf16)] * CHUNKS
        + [pltpu.VMEM((LINE, side, CAP, part, width), bf16)] * (2 * CHUNKS)
        + [pltpu.VMEM((2, hops, owned, part, width), bf16)] * (2 * CHUNKS),
        compiler_params=pltpu.CompilerParams(
            collective_id=0, has_side_effects=True, vmem_limit_bytes=60 * 2**20
        ),
        cost_estimate=pl.CostEstimate(
            flops=flops, bytes_accessed=10 * 2**20, transcendentals=0
        ),
    )(
        source_owner.reshape(-1),
        source_slot,
        target_owner.reshape(-1),
        target_slot,
        wave_blocks,
        davidson_basis,
        left_env,
        right_env,
    )


def solution(mesh):
    return jax.shard_map(
        shards,
        mesh=mesh,
        in_specs=(
            P(("groups", "sector"), None, None),
            P(None, ("groups", "sector"), None, None),
            P(("groups", "sector"), None, None, None),
            P(("groups", "sector"), None, None, None),
            P("groups", None),
            P("groups"),
            P("groups", None),
            P("groups"),
        ),
        out_specs=(P(("groups", "sector"), None, None), P("groups")),
        check_vma=False,
    )
```

```python
import functools

import jax
import jax.numpy as jnp
from jax import lax
from jax.experimental import pallas as pl
from jax.experimental.pallas import tpu as pltpu
from jax.sharding import PartitionSpec as P

CAP = 2
CHUNKS = 2
MESH = pl.DeviceIdType.MESH


def two_hits(owner_ref, base, rows, who, value, default):
    def step(at, found):
        first, second = found
        row = rows - 1 - at
        hit = owner_ref[base + row] == who
        return jnp.where(hit, value(row), first), jnp.where(hit, first, second)

    start = (jnp.int32(default), jnp.int32(default))
    return lax.fori_loop(0, rows, step, start, unroll=16)


def kernel(
    n,
    repeats,
    sown,
    sslot,
    town,
    tslot,
    wave_hbm,
    dav_hbm,
    left_hbm,
    right_hbm,
    applied_ref,
    corr_ref,
    wave,
    dav,
    raw_r,
    raw_l,
    flat_r,
    flat_l,
    in_send0,
    in_send1,
    in_recv0,
    in_recv1,
    operand,
    contracted,
    res0,
    res1,
    out_send0,
    out_send1,
    out_recv0,
    out_recv1,
    acc,
    corr_part,
    corr_send,
    corr_recv,
    landing,
    take,
    take_far,
    rank_of,
    chosen,
    raw0,
    raw1,
    far_send0,
    far_send1,
    raw_ssem,
    raw_rsem,
    far_ssem,
    load_sem,
    right_sem,
    left_sem,
    in_ssem,
    in_rsem,
    out_ssem,
    out_rsem,
    corr_ssem,
    corr_rsem,
):
    me = lax.axis_index("sector")
    rows = sslot.shape[0] // n
    owned, width = wave.shape[0], wave.shape[1]
    envs = right_hbm.shape[0]
    terms = right_hbm.shape[2]
    nv = dav.shape[0]
    part = width // CHUNKS
    half = n // 2
    mine = me // half
    inner = ((me // (half // 2)) % 3) != 0
    partner = lax.rem(me + half, n)
    raw, far_send = (raw0, raw1), (far_send0, far_send1)
    in_send, in_recv = (in_send0, in_send1), (in_recv0, in_recv1)
    res = (res0, res1)
    out_send, out_recv = (out_send0, out_send1), (out_recv0, out_recv1)

    def peer(t):
        off = n // 2 + (1 - 2 * (t % 2)) * ((t + 1) // 2)
        return lax.rem(me + off, n)

    def source(t):
        off = n // 2 + (1 - 2 * (t % 2)) * ((t + 1) // 2)
        return lax.rem(me - off + n, n)

    load_wave = pltpu.make_async_copy(wave_hbm, wave, load_sem.at[0])
    load_dav = pltpu.make_async_copy(dav_hbm, dav, load_sem.at[1])

    def load_right(b):
        return pltpu.make_async_copy(right_hbm.at[b], raw_r.at[b], right_sem.at[b])

    def load_left(a):
        return pltpu.make_async_copy(left_hbm.at[a], raw_l.at[a], left_sem.at[a])

    barrier = pltpu.get_barrier_semaphore()

    @pl.loop(0, n - 1)
    def _(t):
        pl.semaphore_signal(
            barrier, inc=1, device_id={"sector": peer(t)}, device_id_type=MESH
        )

    load_wave.start()
    for b in range(envs):
        load_right(b).start()
    for a in range(envs):
        load_left(a).start()
    load_dav.start()

    def pick(p, owner):
        return two_hits(sown, p * rows, rows, owner, lambda row: sslot[p * rows + row], 0)

    @pl.loop(0, n)
    def _(p):
        for k, slot in enumerate(pick(p, me)):
            take[p * CAP + k] = slot

    load_wave.wait()

    for k in range(CAP):
        slot = take[me * CAP + k]
        for q in range(CHUNKS):
            in_recv[q][me, k] = wave[slot, q * part : (q + 1) * part, :]

    @pl.loop(0, n - 1)
    def _(t):
        p = peer(t)
        for k in range(CAP):
            slot = take[p * CAP + k]
            for q in range(CHUNKS):
                in_send[q][p, k] = wave[slot, q * part : (q + 1) * part, :]

    def in_copy(q, to, frm):
        return pltpu.make_async_remote_copy(
            src_ref=in_send[q].at[to],
            dst_ref=in_recv[q].at[frm],
            send_sem=in_ssem.at[q, to],
            recv_sem=in_rsem.at[q, frm],
            device_id={"sector": to},
            device_id_type=MESH,
        )

    def raw_copy(q):
        return pltpu.make_async_remote_copy(
            src_ref=wave.at[:, q * part : (q + 1) * part, :],
            dst_ref=raw[q],
            send_sem=raw_ssem.at[q],
            recv_sem=raw_rsem.at[q],
            device_id={"sector": partner},
            device_id_type=MESH,
        )

    def far_copy(q, to):
        return pltpu.make_async_remote_copy(
            src_ref=far_send[q].at[to % half],
            dst_ref=in_recv[q].at[partner],
            send_sem=far_ssem.at[q, to % half],
            recv_sem=in_rsem.at[q, partner],
            device_id={"sector": to},
            device_id_type=MESH,
        )

    def direct(p):
        return inner | (p // half == mine)

    def nearby(o):
        return mine * half + lax.rem(me % half + o, half)

    pl.semaphore_wait(barrier, n - 1)

    for q in range(CHUNKS):

        @pl.when(jnp.logical_not(inner))
        def _():
            raw_copy(q).start()

        @pl.loop(0, n - 1)
        def _(t):
            p = peer(t)

            @pl.when(direct(p))
            def _():
                in_copy(q, p, me).start()

    @pl.loop(0, n)
    def _(p):
        for k, slot in enumerate(pick(p, partner)):
            take_far[p * CAP + k] = slot

    def hand_on(q):
        @pl.when(inner)
        def _():
            raw_copy(q).wait_recv()

            @pl.loop(1, half)
            def _(o):
                p = nearby(o)
                for k in range(CAP):
                    far_send[q][p % half, k] = raw[q][take_far[p * CAP + k]]
                far_copy(q, p).start()

            for k in range(CAP):
                in_recv[q][partner, k] = raw[q][take_far[me * CAP + k]]

    tile = 16
    for b in range(envs):
        load_right(b).wait()

    @pl.loop(0, envs * width // tile)
    def _(i):
        b = i // (width // tile)
        r = (i % (width // tile)) * tile
        r = pl.multiple_of(r, tile)
        block = jnp.swapaxes(raw_r[b, pl.ds(r, tile)], 0, 1)
        for w in range(terms):
            flat_r[pl.ds(pl.multiple_of(b * width + r, tile), tile), w * width : (w + 1) * width] = block[w]

    hand_on(0)

    for a in range(envs):
        load_left(a).wait()

    @pl.loop(0, envs * width // tile)
    def _(i):
        a = i // (width // tile)
        x = (i % (width // tile)) * tile
        x = pl.multiple_of(x, tile)
        q = x // part
        block = jnp.swapaxes(raw_l[a, pl.ds(x, tile)], 0, 1)
        at = pl.multiple_of(q * envs * part + a * part + x % part, tile)
        for w in range(terms):
            flat_l[pl.ds(at, tile), w * width : (w + 1) * width] = block[w]

    @pl.loop(0, n)
    def _(j):
        hits = two_hits(town, j * rows, rows, me, lambda row: tslot[j * rows + row], -1)
        for k in range(CAP):
            landing[j * CAP + k] = hits[k]

    hand_on(1)
    acc[...] = jnp.zeros_like(acc)
    load_dav.wait()

    @pl.loop(0, rows)
    def _(i):
        owner = sown[me * rows + i]

        def count(h, seen):
            same = (sown[me * rows + h] == owner) & (h < i)
            return seen + same.astype(jnp.int32)

        rank = lax.fori_loop(0, rows, count, jnp.int32(0), unroll=16)
        rank_of[i] = owner * CAP + jnp.minimum(rank, CAP - 1)

    @pl.loop(0, n)
    def _(p):
        hits = two_hits(town, me * rows, rows, p, lambda row: row, 0)
        for k in range(CAP):
            chosen[p * CAP + k] = hits[k]

    for q in range(CHUNKS):

        @pl.loop(0, n - 1)
        def _(t):
            owner = source(t)

            @pl.when(jnp.logical_not(inner & (owner == partner)))
            def _():
                in_copy(q, owner, owner).wait_recv()

        @pl.loop(0, rows)
        def _(i):
            at = rank_of[i]
            b = i // repeats
            c = i % repeats
            operand[
                pl.ds(pl.multiple_of(c * part, part), part),
                pl.ds(pl.multiple_of(b * width, width), width),
            ] = in_recv[q][at // CAP, at % CAP]

        @pl.loop(0, terms // 2)
        def _(pair):
            cols = pl.ds(pl.multiple_of(pair * 2 * width, 2 * width), 2 * width)
            out = jnp.dot(
                operand[...], flat_r[:, cols], preferred_element_type=jnp.float32
            ).astype(jnp.bfloat16)
            for c in range(repeats):
                for h in range(2):
                    at = pl.multiple_of((pair * 2 + h) * width + q * part, part)
                    contracted[pl.ds(at, part), c * width : (c + 1) * width] = out[
                        c * part : (c + 1) * part, h * width : (h + 1) * width
                    ]

    def out_copy(q, to, frm):
        return pltpu.make_async_remote_copy(
            src_ref=out_send[q].at[to],
            dst_ref=out_recv[q].at[frm],
            send_sem=out_ssem.at[q, to],
            recv_sem=out_rsem.at[q, frm],
            device_id={"sector": to},
            device_id_type=MESH,
        )

    for q in range(CHUNKS):
        lhs_rows = slice(q * envs * part, (q + 1) * envs * part)

        @pl.loop(0, repeats // 2)
        def _(pair):
            cols = pl.ds(pl.multiple_of(pair * 2 * width, 2 * width), 2 * width)
            out = jnp.dot(
                flat_l[lhs_rows, :], contracted[:, cols], preferred_element_type=jnp.float32
            ).astype(jnp.bfloat16)
            for a in range(envs):
                for h in range(2):
                    res[q][a * repeats + pair * 2 + h] = out[
                        a * part : (a + 1) * part, h * width : (h + 1) * width
                    ]

        @pl.loop(0, n - 1)
        def _(t):
            p = peer(t)
            for k in range(CAP):
                out_send[q][p, k] = res[q][chosen[p * CAP + k]]
            out_copy(q, p, me).start()

        for k in range(CAP):
            out_recv[q][me, k] = res[q][chosen[me * CAP + k]]

    def add(q, j):
        values = [out_recv[q][j, k].astype(jnp.float32) for k in range(CAP)]
        lands = [landing[j * CAP + k] for k in range(CAP)]
        for d in range(owned):
            total = acc[q, d]
            for k in range(CAP):
                total = total + jnp.where(lands[k] == d, 1.0, 0.0) * values[k]
            acc[q, d] = total

    partial = [jnp.zeros((8, width), jnp.float32) for _ in range(nv)]
    for q in range(CHUNKS):
        add(q, me)

        @pl.loop(0, n - 1)
        def _(t):
            j = source(t)
            out_copy(q, j, j).wait_recv()
            add(q, j)

        for d in range(owned):
            block = acc[q, d].astype(jnp.bfloat16)
            applied_ref[d, q * part : (q + 1) * part, :] = block
            block = block.astype(jnp.float32)
            for v in range(nv):
                prod = dav[v, d, q * part : (q + 1) * part, :].astype(jnp.float32) * block
                partial[v] = partial[v] + jnp.sum(prod.reshape(part // 8, 8, width), axis=0)

    for v in range(nv):
        corr_send[v : v + 1, :] = jnp.sum(partial[v], axis=0, keepdims=True)
    if nv < corr_send.shape[0]:
        corr_send[nv:, :] = jnp.zeros((corr_send.shape[0] - nv, width), jnp.float32)

    def corr_copy(to, frm):
        return pltpu.make_async_remote_copy(
            src_ref=corr_send,
            dst_ref=corr_recv.at[frm],
            send_sem=corr_ssem.at[to],
            recv_sem=corr_rsem.at[frm],
            device_id={"sector": to},
            device_id_type=MESH,
        )

    @pl.loop(0, n - 1)
    def _(t):
        corr_copy(peer(t), me).start()

    corr_recv[me] = corr_send[...]

    @pl.loop(0, n - 1)
    def _(t):
        p = peer(t)
        for q in range(CHUNKS):
            out_copy(q, p, me).wait_send()

            @pl.when(direct(p))
            def _():
                in_copy(q, p, me).wait_send()

    for q in range(CHUNKS):

        @pl.when(jnp.logical_not(inner))
        def _():
            raw_copy(q).wait_send()

        @pl.when(inner)
        def _():
            @pl.loop(1, half)
            def _(o):
                far_copy(q, nearby(o)).wait_send()

    @pl.loop(0, n - 1)
    def _(t):
        corr_copy(source(t), source(t)).wait_recv()

    total = jnp.sum(corr_recv[...], axis=0)
    for v in range(nv):
        corr_ref[v] = jnp.sum(total[v : v + 1, :])

    @pl.loop(0, n - 1)
    def _(t):
        corr_copy(peer(t), me).wait_send()


def shards(
    wave_blocks,
    davidson_basis,
    left_env,
    right_env,
    source_owner,
    source_slot,
    target_owner,
    target_slot,
):
    n = lax.axis_size("sector")
    owned, width = wave_blocks.shape[0], wave_blocks.shape[1]
    envs, terms = right_env.shape[0], right_env.shape[2]
    rows = source_slot.shape[0] // n
    repeats = rows // envs
    nv = davidson_basis.shape[0]
    part = width // CHUNKS
    corr_rows = -(-nv // 8) * 8
    bf16 = jnp.bfloat16
    smem = pl.BlockSpec(memory_space=pltpu.SMEM)
    vmem = pl.BlockSpec(memory_space=pltpu.VMEM)
    hbm = pl.BlockSpec(memory_space=pl.ANY)
    dma = pltpu.SemaphoreType.DMA
    flops = 4 * rows * terms * width**3
    return pl.pallas_call(
        functools.partial(kernel, n, repeats),
        out_shape=(
            jax.ShapeDtypeStruct((owned, width, width), bf16),
            jax.ShapeDtypeStruct((nv,), jnp.float32),
        ),
        in_specs=[smem] * 4 + [hbm] * 4,
        out_specs=(vmem, smem),
        scratch_shapes=[
            pltpu.VMEM((owned, width, width), bf16),
            pltpu.VMEM((nv, owned, width, width), bf16),
            pltpu.VMEM((envs, width, terms, width), bf16),
            pltpu.VMEM((envs, width, terms, width), bf16),
            pltpu.VMEM((envs * width, terms * width), bf16),
            pltpu.VMEM((envs * width, terms * width), bf16),
            pltpu.VMEM((n, CAP, part, width), bf16),
            pltpu.VMEM((n, CAP, part, width), bf16),
            pltpu.VMEM((n, CAP, part, width), bf16),
            pltpu.VMEM((n, CAP, part, width), bf16),
            pltpu.VMEM((repeats * part, envs * width), bf16),
            pltpu.VMEM((terms * width, repeats * width), bf16),
            pltpu.VMEM((rows, part, width), bf16),
            pltpu.VMEM((rows, part, width), bf16),
            pltpu.VMEM((n, CAP, part, width), bf16),
            pltpu.VMEM((n, CAP, part, width), bf16),
            pltpu.VMEM((n, CAP, part, width), bf16),
            pltpu.VMEM((n, CAP, part, width), bf16),
            pltpu.VMEM((CHUNKS, owned, part, width), jnp.float32),
            pltpu.VMEM((nv, 8, width), jnp.float32),
            pltpu.VMEM((corr_rows, width), jnp.float32),
            pltpu.VMEM((n, corr_rows, width), jnp.float32),
            pltpu.SMEM((n * CAP,), jnp.int32),
            pltpu.SMEM((n * CAP,), jnp.int32),
            pltpu.SMEM((n * CAP,), jnp.int32),
            pltpu.SMEM((rows,), jnp.int32),
            pltpu.SMEM((n * CAP,), jnp.int32),
            pltpu.VMEM((owned, part, width), bf16),
            pltpu.VMEM((owned, part, width), bf16),
            pltpu.VMEM((n // 2, CAP, part, width), bf16),
            pltpu.VMEM((n // 2, CAP, part, width), bf16),
            dma((CHUNKS,)),
            dma((CHUNKS,)),
            dma((CHUNKS, n // 2)),
            dma((2,)),
            dma((envs,)),
            dma((envs,)),
            dma((CHUNKS, n)),
            dma((CHUNKS, n)),
            dma((CHUNKS, n)),
            dma((CHUNKS, n)),
            dma((n,)),
            dma((n,)),
        ],
        compiler_params=pltpu.CompilerParams(
            collective_id=0, has_side_effects=True, vmem_limit_bytes=60 * 2**20
        ),
        cost_estimate=pl.CostEstimate(
            flops=flops, bytes_accessed=10 * 2**20, transcendentals=0
        ),
    )(
        source_owner.reshape(-1),
        source_slot,
        target_owner.reshape(-1),
        target_slot,
        wave_blocks,
        davidson_basis,
        left_env,
        right_env,
    )


def solution(mesh):
    return jax.shard_map(
        shards,
        mesh=mesh,
        in_specs=(
            P(("groups", "sector"), None, None),
            P(None, ("groups", "sector"), None, None),
            P(("groups", "sector"), None, None, None),
            P(("groups", "sector"), None, None, None),
            P("groups", None),
            P("groups"),
            P("groups", None),
            P("groups"),
        ),
        out_specs=(P(("groups", "sector"), None, None), P("groups")),
        check_vma=False,
    )
```

```python
import functools

import jax
import jax.numpy as jnp
from jax import lax
from jax.experimental import pallas as pl
from jax.experimental.pallas import tpu as pltpu
from jax.sharding import PartitionSpec as P

CAP = 2
CHUNKS = 2
MESH = pl.DeviceIdType.MESH


def two_hits(owner_ref, base, rows, who, value, default):
    def step(at, found):
        first, second = found
        row = rows - 1 - at
        hit = owner_ref[base + row] == who
        return jnp.where(hit, value(row), first), jnp.where(hit, first, second)

    start = (jnp.int32(default), jnp.int32(default))
    return lax.fori_loop(0, rows, step, start, unroll=16)


def kernel(
    n,
    repeats,
    sown,
    sslot,
    town,
    tslot,
    wave_hbm,
    dav_hbm,
    left_hbm,
    right_hbm,
    applied_ref,
    corr_ref,
    wave,
    dav,
    raw_r,
    raw_l,
    flat_r,
    flat_l,
    in_send0,
    in_send1,
    in_recv0,
    in_recv1,
    operand,
    contracted,
    res0,
    res1,
    out_send0,
    out_send1,
    out_recv0,
    out_recv1,
    acc,
    corr_part,
    corr_send,
    corr_recv,
    landing,
    take,
    take_far,
    rank_of,
    chosen,
    raw0,
    raw1,
    far_send0,
    far_send1,
    raw_ssem,
    raw_rsem,
    far_ssem,
    gath0,
    gath1,
    sum_send0,
    sum_send1,
    sum_recv0,
    sum_recv1,
    landing_far,
    gath_rsem,
    sum_ssem,
    sum_rsem,
    load_sem,
    right_sem,
    left_sem,
    in_ssem,
    in_rsem,
    out_ssem,
    out_rsem,
    corr_ssem,
    corr_rsem,
):
    me = lax.axis_index("sector")
    rows = sslot.shape[0] // n
    owned, width = wave.shape[0], wave.shape[1]
    envs = right_hbm.shape[0]
    terms = right_hbm.shape[2]
    nv = dav.shape[0]
    part = width // CHUNKS
    half = n // 2
    mine = me // half
    inner = ((me // (half // 2)) % 3) != 0
    partner = lax.rem(me + half, n)
    gath, sum_send, sum_recv = (gath0, gath1), (sum_send0, sum_send1), (sum_recv0, sum_recv1)
    raw, far_send = (raw0, raw1), (far_send0, far_send1)
    in_send, in_recv = (in_send0, in_send1), (in_recv0, in_recv1)
    res = (res0, res1)
    out_send, out_recv = (out_send0, out_send1), (out_recv0, out_recv1)

    def peer(t):
        off = n // 2 + (1 - 2 * (t % 2)) * ((t + 1) // 2)
        return lax.rem(me + off, n)

    def source(t):
        off = n // 2 + (1 - 2 * (t % 2)) * ((t + 1) // 2)
        return lax.rem(me - off + n, n)

    load_wave = pltpu.make_async_copy(wave_hbm, wave, load_sem.at[0])
    load_dav = pltpu.make_async_copy(dav_hbm, dav, load_sem.at[1])

    def load_right(b):
        return pltpu.make_async_copy(right_hbm.at[b], raw_r.at[b], right_sem.at[b])

    def load_left(a):
        return pltpu.make_async_copy(left_hbm.at[a], raw_l.at[a], left_sem.at[a])

    barrier = pltpu.get_barrier_semaphore()

    @pl.loop(0, n - 1)
    def _(t):
        pl.semaphore_signal(
            barrier, inc=1, device_id={"sector": peer(t)}, device_id_type=MESH
        )

    load_wave.start()
    for b in range(envs):
        load_right(b).start()
    for a in range(envs):
        load_left(a).start()
    load_dav.start()

    def pick(p, owner):
        return two_hits(sown, p * rows, rows, owner, lambda row: sslot[p * rows + row], 0)

    @pl.loop(0, n)
    def _(p):
        for k, slot in enumerate(pick(p, me)):
            take[p * CAP + k] = slot

    load_wave.wait()

    for k in range(CAP):
        slot = take[me * CAP + k]
        for q in range(CHUNKS):
            in_recv[q][me, k] = wave[slot, q * part : (q + 1) * part, :]

    @pl.loop(0, n - 1)
    def _(t):
        p = peer(t)
        for k in range(CAP):
            slot = take[p * CAP + k]
            for q in range(CHUNKS):
                in_send[q][p, k] = wave[slot, q * part : (q + 1) * part, :]

    def in_copy(q, to, frm):
        return pltpu.make_async_remote_copy(
            src_ref=in_send[q].at[to],
            dst_ref=in_recv[q].at[frm],
            send_sem=in_ssem.at[q, to],
            recv_sem=in_rsem.at[q, frm],
            device_id={"sector": to},
            device_id_type=MESH,
        )

    def raw_copy(q):
        return pltpu.make_async_remote_copy(
            src_ref=wave.at[:, q * part : (q + 1) * part, :],
            dst_ref=raw[q],
            send_sem=raw_ssem.at[q],
            recv_sem=raw_rsem.at[q],
            device_id={"sector": partner},
            device_id_type=MESH,
        )

    def far_copy(q, to):
        return pltpu.make_async_remote_copy(
            src_ref=far_send[q].at[to % half],
            dst_ref=in_recv[q].at[partner],
            send_sem=far_ssem.at[q, to % half],
            recv_sem=in_rsem.at[q, partner],
            device_id={"sector": to},
            device_id_type=MESH,
        )

    def direct(p):
        return inner | (p // half == mine)

    def nearby(o):
        return mine * half + lax.rem(me % half + o, half)

    pl.semaphore_wait(barrier, n - 1)

    for q in range(CHUNKS):

        @pl.when(jnp.logical_not(inner))
        def _():
            raw_copy(q).start()

        @pl.loop(0, n - 1)
        def _(t):
            p = peer(t)

            @pl.when(direct(p))
            def _():
                in_copy(q, p, me).start()

    @pl.loop(0, n)
    def _(p):
        for k, slot in enumerate(pick(p, partner)):
            take_far[p * CAP + k] = slot

    def hand_on(q):
        @pl.when(inner)
        def _():
            raw_copy(q).wait_recv()

            @pl.loop(1, half)
            def _(o):
                p = nearby(o)
                for k in range(CAP):
                    far_send[q][p % half, k] = raw[q][take_far[p * CAP + k]]
                far_copy(q, p).start()

            for k in range(CAP):
                in_recv[q][partner, k] = raw[q][take_far[me * CAP + k]]

    tile = 16
    for b in range(envs):
        load_right(b).wait()

    @pl.loop(0, envs * width // tile)
    def _(i):
        b = i // (width // tile)
        r = (i % (width // tile)) * tile
        r = pl.multiple_of(r, tile)
        block = jnp.swapaxes(raw_r[b, pl.ds(r, tile)], 0, 1)
        for w in range(terms):
            flat_r[pl.ds(pl.multiple_of(b * width + r, tile), tile), w * width : (w + 1) * width] = block[w]

    hand_on(0)

    for a in range(envs):
        load_left(a).wait()

    @pl.loop(0, envs * width // tile)
    def _(i):
        a = i // (width // tile)
        x = (i % (width // tile)) * tile
        x = pl.multiple_of(x, tile)
        q = x // part
        block = jnp.swapaxes(raw_l[a, pl.ds(x, tile)], 0, 1)
        at = pl.multiple_of(q * envs * part + a * part + x % part, tile)
        for w in range(terms):
            flat_l[pl.ds(at, tile), w * width : (w + 1) * width] = block[w]

    @pl.loop(0, n)
    def _(j):
        hits = two_hits(town, j * rows, rows, me, lambda row: tslot[j * rows + row], -1)
        for k in range(CAP):
            landing[j * CAP + k] = hits[k]

    @pl.loop(0, half)
    def _(h):
        base = (mine * half + h) * rows
        hits = two_hits(town, base, rows, partner, lambda row: tslot[base + row], -1)
        for k in range(CAP):
            landing_far[h * CAP + k] = hits[k]

    hand_on(1)
    acc[...] = jnp.zeros_like(acc)
    load_dav.wait()

    @pl.loop(0, rows)
    def _(i):
        owner = sown[me * rows + i]

        def count(h, seen):
            same = (sown[me * rows + h] == owner) & (h < i)
            return seen + same.astype(jnp.int32)

        rank = lax.fori_loop(0, rows, count, jnp.int32(0), unroll=16)
        rank_of[i] = owner * CAP + jnp.minimum(rank, CAP - 1)

    @pl.loop(0, n)
    def _(p):
        hits = two_hits(town, me * rows, rows, p, lambda row: row, 0)
        for k in range(CAP):
            chosen[p * CAP + k] = hits[k]

    for q in range(CHUNKS):

        @pl.loop(0, n - 1)
        def _(t):
            owner = source(t)

            @pl.when(jnp.logical_not(inner & (owner == partner)))
            def _():
                in_copy(q, owner, owner).wait_recv()

        @pl.loop(0, rows)
        def _(i):
            at = rank_of[i]
            b = i // repeats
            c = i % repeats
            operand[
                pl.ds(pl.multiple_of(c * part, part), part),
                pl.ds(pl.multiple_of(b * width, width), width),
            ] = in_recv[q][at // CAP, at % CAP]

        @pl.loop(0, terms // 2)
        def _(pair):
            cols = pl.ds(pl.multiple_of(pair * 2 * width, 2 * width), 2 * width)
            out = jnp.dot(
                operand[...], flat_r[:, cols], preferred_element_type=jnp.float32
            ).astype(jnp.bfloat16)
            for c in range(repeats):
                for h in range(2):
                    at = pl.multiple_of((pair * 2 + h) * width + q * part, part)
                    contracted[pl.ds(at, part), c * width : (c + 1) * width] = out[
                        c * part : (c + 1) * part, h * width : (h + 1) * width
                    ]

    def out_copy(q, to, frm):
        return pltpu.make_async_remote_copy(
            src_ref=out_send[q].at[to],
            dst_ref=out_recv[q].at[frm],
            send_sem=out_ssem.at[q, to],
            recv_sem=out_rsem.at[q, frm],
            device_id={"sector": to},
            device_id_type=MESH,
        )

    def gather_copy(q, p, to, frm):
        return pltpu.make_async_remote_copy(
            src_ref=out_send[q].at[p],
            dst_ref=gath[q].at[frm],
            send_sem=out_ssem.at[q, p],
            recv_sem=gath_rsem.at[q, frm],
            device_id={"sector": to},
            device_id_type=MESH,
        )

    def sum_copy(q):
        return pltpu.make_async_remote_copy(
            src_ref=sum_send[q],
            dst_ref=sum_recv[q],
            send_sem=sum_ssem.at[q],
            recv_sem=sum_rsem.at[q],
            device_id={"sector": partner},
            device_id_type=MESH,
        )

    quarter = half // 2
    far_end = jnp.where(mine == 0, 3, 0) * quarter

    def reached(p):
        return (p // half == mine) | ((p // quarter) % 3 != 0)

    for q in range(CHUNKS):
        lhs_rows = slice(q * envs * part, (q + 1) * envs * part)

        @pl.loop(0, repeats // 2)
        def _(pair):
            cols = pl.ds(pl.multiple_of(pair * 2 * width, 2 * width), 2 * width)
            out = jnp.dot(
                flat_l[lhs_rows, :], contracted[:, cols], preferred_element_type=jnp.float32
            ).astype(jnp.bfloat16)
            for a in range(envs):
                for h in range(2):
                    res[q][a * repeats + pair * 2 + h] = out[
                        a * part : (a + 1) * part, h * width : (h + 1) * width
                    ]

        @pl.loop(0, quarter)
        def _(i):
            p = far_end + i
            to = lax.rem(p + half, n)
            for k in range(CAP):
                out_send[q][p, k] = res[q][chosen[p * CAP + k]]

            @pl.when(to != me)
            def _():
                gather_copy(q, p, to, me % half).start()

        @pl.when(inner)
        def _():
            for k in range(CAP):
                gath[q][me % half, k] = res[q][chosen[partner * CAP + k]]

        @pl.loop(0, n - 1)
        def _(t):
            p = peer(t)

            @pl.when(reached(p))
            def _():
                for k in range(CAP):
                    out_send[q][p, k] = res[q][chosen[p * CAP + k]]
                out_copy(q, p, me).start()

        for k in range(CAP):
            out_recv[q][me, k] = res[q][chosen[me * CAP + k]]

    tile = 16
    for q in range(CHUNKS):

        @pl.when(inner)
        def _():
            @pl.loop(1, half)
            def _(o):
                frm = lax.rem(me % half + o, half)
                gather_copy(q, partner, me, frm).wait_recv()

            @pl.loop(0, part // tile)
            def _(i):
                at = pl.ds(pl.multiple_of(i * tile, tile), tile)

                def gather(frm, totals):
                    totals = list(totals)
                    for k in range(CAP):
                        value = gath[q][frm, k, at].astype(jnp.float32)
                        land = landing_far[frm * CAP + k]
                        for b in range(owned):
                            totals[b] = totals[b] + jnp.where(land == b, 1.0, 0.0) * value
                    return tuple(totals)

                zero = tuple(jnp.zeros((tile, width), jnp.float32) for _ in range(owned))
                totals = lax.fori_loop(0, half, gather, zero, unroll=4)
                for b in range(owned):
                    sum_send[q][b, at] = totals[b].astype(jnp.bfloat16)

            sum_copy(q).start()

    def add(q, j):
        values = [out_recv[q][j, k].astype(jnp.float32) for k in range(CAP)]
        lands = [landing[j * CAP + k] for k in range(CAP)]
        for d in range(owned):
            total = acc[q, d]
            for k in range(CAP):
                total = total + jnp.where(lands[k] == d, 1.0, 0.0) * values[k]
            acc[q, d] = total

    partial = [jnp.zeros((8, width), jnp.float32) for _ in range(nv)]
    for q in range(CHUNKS):
        add(q, me)

        @pl.loop(0, n - 1)
        def _(t):
            j = source(t)

            @pl.when(direct(j))
            def _():
                out_copy(q, j, j).wait_recv()
                add(q, j)

        @pl.when(jnp.logical_not(inner))
        def _():
            sum_copy(q).wait_recv()

            @pl.loop(0, owned)
            def _(d):
                acc[q, d] = acc[q, d] + sum_recv[q][d].astype(jnp.float32)

        for d in range(owned):
            block = acc[q, d].astype(jnp.bfloat16)
            applied_ref[d, q * part : (q + 1) * part, :] = block
            block = block.astype(jnp.float32)
            for v in range(nv):
                prod = dav[v, d, q * part : (q + 1) * part, :].astype(jnp.float32) * block
                partial[v] = partial[v] + jnp.sum(prod.reshape(part // 8, 8, width), axis=0)

    for v in range(nv):
        corr_send[v : v + 1, :] = jnp.sum(partial[v], axis=0, keepdims=True)
    if nv < corr_send.shape[0]:
        corr_send[nv:, :] = jnp.zeros((corr_send.shape[0] - nv, width), jnp.float32)

    def corr_copy(to, frm):
        return pltpu.make_async_remote_copy(
            src_ref=corr_send,
            dst_ref=corr_recv.at[frm],
            send_sem=corr_ssem.at[to],
            recv_sem=corr_rsem.at[frm],
            device_id={"sector": to},
            device_id_type=MESH,
        )

    @pl.loop(0, n - 1)
    def _(t):
        corr_copy(peer(t), me).start()

    corr_recv[me] = corr_send[...]

    @pl.loop(0, n - 1)
    def _(t):
        p = peer(t)
        for q in range(CHUNKS):

            @pl.when(reached(p) | (lax.rem(p + half, n) != me))
            def _():
                out_copy(q, p, me).wait_send()

            @pl.when(direct(p))
            def _():
                in_copy(q, p, me).wait_send()

    for q in range(CHUNKS):

        @pl.when(jnp.logical_not(inner))
        def _():
            raw_copy(q).wait_send()

        @pl.when(inner)
        def _():
            sum_copy(q).wait_send()

        @pl.when(inner)
        def _():
            @pl.loop(1, half)
            def _(o):
                far_copy(q, nearby(o)).wait_send()

    @pl.loop(0, n - 1)
    def _(t):
        corr_copy(source(t), source(t)).wait_recv()

    total = jnp.sum(corr_recv[...], axis=0)
    for v in range(nv):
        corr_ref[v] = jnp.sum(total[v : v + 1, :])

    @pl.loop(0, n - 1)
    def _(t):
        corr_copy(peer(t), me).wait_send()


def shards(
    wave_blocks,
    davidson_basis,
    left_env,
    right_env,
    source_owner,
    source_slot,
    target_owner,
    target_slot,
):
    n = lax.axis_size("sector")
    owned, width = wave_blocks.shape[0], wave_blocks.shape[1]
    envs, terms = right_env.shape[0], right_env.shape[2]
    rows = source_slot.shape[0] // n
    repeats = rows // envs
    nv = davidson_basis.shape[0]
    part = width // CHUNKS
    corr_rows = -(-nv // 8) * 8
    bf16 = jnp.bfloat16
    smem = pl.BlockSpec(memory_space=pltpu.SMEM)
    vmem = pl.BlockSpec(memory_space=pltpu.VMEM)
    hbm = pl.BlockSpec(memory_space=pl.ANY)
    dma = pltpu.SemaphoreType.DMA
    flops = 4 * rows * terms * width**3
    return pl.pallas_call(
        functools.partial(kernel, n, repeats),
        out_shape=(
            jax.ShapeDtypeStruct((owned, width, width), bf16),
            jax.ShapeDtypeStruct((nv,), jnp.float32),
        ),
        in_specs=[smem] * 4 + [hbm] * 4,
        out_specs=(vmem, smem),
        scratch_shapes=[
            pltpu.VMEM((owned, width, width), bf16),
            pltpu.VMEM((nv, owned, width, width), bf16),
            pltpu.VMEM((envs, width, terms, width), bf16),
            pltpu.VMEM((envs, width, terms, width), bf16),
            pltpu.VMEM((envs * width, terms * width), bf16),
            pltpu.VMEM((envs * width, terms * width), bf16),
            pltpu.VMEM((n, CAP, part, width), bf16),
            pltpu.VMEM((n, CAP, part, width), bf16),
            pltpu.VMEM((n, CAP, part, width), bf16),
            pltpu.VMEM((n, CAP, part, width), bf16),
            pltpu.VMEM((repeats * part, envs * width), bf16),
            pltpu.VMEM((terms * width, repeats * width), bf16),
            pltpu.VMEM((rows, part, width), bf16),
            pltpu.VMEM((rows, part, width), bf16),
            pltpu.VMEM((n, CAP, part, width), bf16),
            pltpu.VMEM((n, CAP, part, width), bf16),
            pltpu.VMEM((n, CAP, part, width), bf16),
            pltpu.VMEM((n, CAP, part, width), bf16),
            pltpu.VMEM((CHUNKS, owned, part, width), jnp.float32),
            pltpu.VMEM((nv, 8, width), jnp.float32),
            pltpu.VMEM((corr_rows, width), jnp.float32),
            pltpu.VMEM((n, corr_rows, width), jnp.float32),
            pltpu.SMEM((n * CAP,), jnp.int32),
            pltpu.SMEM((n * CAP,), jnp.int32),
            pltpu.SMEM((n * CAP,), jnp.int32),
            pltpu.SMEM((rows,), jnp.int32),
            pltpu.SMEM((n * CAP,), jnp.int32),
            pltpu.VMEM((owned, part, width), bf16),
            pltpu.VMEM((owned, part, width), bf16),
            pltpu.VMEM((n // 2, CAP, part, width), bf16),
            pltpu.VMEM((n // 2, CAP, part, width), bf16),
            dma((CHUNKS,)),
            dma((CHUNKS,)),
            dma((CHUNKS, n // 2)),
            pltpu.VMEM((n // 2, CAP, part, width), bf16),
            pltpu.VMEM((n // 2, CAP, part, width), bf16),
            pltpu.VMEM((owned, part, width), bf16),
            pltpu.VMEM((owned, part, width), bf16),
            pltpu.VMEM((owned, part, width), bf16),
            pltpu.VMEM((owned, part, width), bf16),
            pltpu.SMEM((n // 2 * CAP,), jnp.int32),
            dma((CHUNKS, n // 2)),
            dma((CHUNKS,)),
            dma((CHUNKS,)),
            dma((2,)),
            dma((envs,)),
            dma((envs,)),
            dma((CHUNKS, n)),
            dma((CHUNKS, n)),
            dma((CHUNKS, n)),
            dma((CHUNKS, n)),
            dma((n,)),
            dma((n,)),
        ],
        compiler_params=pltpu.CompilerParams(
            collective_id=0, has_side_effects=True, vmem_limit_bytes=60 * 2**20
        ),
        cost_estimate=pl.CostEstimate(
            flops=flops, bytes_accessed=10 * 2**20, transcendentals=0
        ),
    )(
        source_owner.reshape(-1),
        source_slot,
        target_owner.reshape(-1),
        target_slot,
        wave_blocks,
        davidson_basis,
        left_env,
        right_env,
    )


def solution(mesh):
    return jax.shard_map(
        shards,
        mesh=mesh,
        in_specs=(
            P(("groups", "sector"), None, None),
            P(None, ("groups", "sector"), None, None),
            P(("groups", "sector"), None, None, None),
            P(("groups", "sector"), None, None, None),
            P("groups", None),
            P("groups"),
            P("groups", None),
            P("groups"),
        ),
        out_specs=(P(("groups", "sector"), None, None), P("groups")),
        check_vma=False,
    )
```

```python
import functools

import jax
import jax.numpy as jnp
from jax import lax
from jax.experimental import pallas as pl
from jax.experimental.pallas import tpu as pltpu
from jax.sharding import PartitionSpec as P

CAP = 2
CHUNKS = 2
MESH = pl.DeviceIdType.MESH


def two_hits(owner_ref, base, rows, who, value, default):
    def step(at, found):
        first, second = found
        row = rows - 1 - at
        hit = owner_ref[base + row] == who
        return jnp.where(hit, value(row), first), jnp.where(hit, first, second)

    start = (jnp.int32(default), jnp.int32(default))
    return lax.fori_loop(0, rows, step, start, unroll=16)


def kernel(
    n,
    repeats,
    sown_hbm,
    sslot_hbm,
    town_hbm,
    tslot_hbm,
    wave_hbm,
    dav_hbm,
    left_hbm,
    right_hbm,
    applied_hbm,
    corr_ref,
    sown,
    sslot,
    town,
    tslot,
    applied_ref,
    table_sem,
    store_sem,
    wave,
    dav,
    raw_r,
    raw_l,
    flat_r,
    flat_l,
    in_send0,
    in_send1,
    in_recv0,
    in_recv1,
    operand,
    contracted,
    res0,
    res1,
    out_send0,
    out_send1,
    out_recv0,
    out_recv1,
    acc,
    corr_part,
    corr_send,
    corr_recv,
    landing,
    take,
    take_far,
    rank_of,
    chosen,
    raw0,
    raw1,
    far_send0,
    far_send1,
    raw_ssem,
    raw_rsem,
    far_ssem,
    gath0,
    gath1,
    sum_send0,
    sum_send1,
    sum_recv0,
    sum_recv1,
    landing_far,
    gath_rsem,
    sum_ssem,
    sum_rsem,
    load_sem,
    right_sem,
    left_sem,
    in_ssem,
    in_rsem,
    out_ssem,
    out_rsem,
    corr_ssem,
    corr_rsem,
):
    me = lax.axis_index("sector")
    rows = sslot.shape[0] // n
    owned, width = wave.shape[0], wave.shape[1]
    envs = right_hbm.shape[0]
    terms = right_hbm.shape[2]
    nv = dav.shape[0]
    part = width // CHUNKS
    half = n // 2
    mine = me // half
    inner = ((me // (half // 2)) % 3) != 0
    partner = lax.rem(me + half, n)
    gath, sum_send, sum_recv = (gath0, gath1), (sum_send0, sum_send1), (sum_recv0, sum_recv1)
    raw, far_send = (raw0, raw1), (far_send0, far_send1)
    in_send, in_recv = (in_send0, in_send1), (in_recv0, in_recv1)
    res = (res0, res1)
    out_send, out_recv = (out_send0, out_send1), (out_recv0, out_recv1)

    def peer(t):
        off = n // 2 + (1 - 2 * (t % 2)) * ((t + 1) // 2)
        return lax.rem(me + off, n)

    def source(t):
        off = n // 2 + (1 - 2 * (t % 2)) * ((t + 1) // 2)
        return lax.rem(me - off + n, n)

    load_wave = pltpu.make_async_copy(wave_hbm, wave, load_sem.at[0])
    load_dav = pltpu.make_async_copy(dav_hbm, dav, load_sem.at[1])

    def load_right(b):
        return pltpu.make_async_copy(right_hbm.at[b], raw_r.at[b], right_sem.at[b])

    def load_left(a):
        return pltpu.make_async_copy(left_hbm.at[a], raw_l.at[a], left_sem.at[a])

    barrier = pltpu.get_barrier_semaphore()

    @pl.loop(0, n - 1)
    def _(t):
        pl.semaphore_signal(
            barrier, inc=1, device_id={"sector": peer(t)}, device_id_type=MESH
        )

    tables = [
        pltpu.make_async_copy(src, dst, table_sem.at[at])
        for at, (src, dst) in enumerate(
            ((sown_hbm, sown), (sslot_hbm, sslot), (town_hbm, town), (tslot_hbm, tslot))
        )
    ]
    for table in tables:
        table.start()
    load_wave.start()
    for b in range(envs):
        load_right(b).start()
    for a in range(envs):
        load_left(a).start()
    load_dav.start()

    def pick(p, owner):
        return two_hits(sown, p * rows, rows, owner, lambda row: sslot[p * rows + row], 0)

    for table in tables:
        table.wait()

    @pl.loop(0, n)
    def _(p):
        for k, slot in enumerate(pick(p, me)):
            take[p * CAP + k] = slot

    load_wave.wait()

    for k in range(CAP):
        slot = take[me * CAP + k]
        for q in range(CHUNKS):
            in_recv[q][me, k] = wave[slot, q * part : (q + 1) * part, :]

    @pl.loop(0, n - 1)
    def _(t):
        p = peer(t)
        for k in range(CAP):
            slot = take[p * CAP + k]
            for q in range(CHUNKS):
                in_send[q][p, k] = wave[slot, q * part : (q + 1) * part, :]

    def in_copy(q, to, frm):
        return pltpu.make_async_remote_copy(
            src_ref=in_send[q].at[to],
            dst_ref=in_recv[q].at[frm],
            send_sem=in_ssem.at[q, to],
            recv_sem=in_rsem.at[q, frm],
            device_id={"sector": to},
            device_id_type=MESH,
        )

    def raw_copy(q):
        return pltpu.make_async_remote_copy(
            src_ref=wave.at[:, q * part : (q + 1) * part, :],
            dst_ref=raw[q],
            send_sem=raw_ssem.at[q],
            recv_sem=raw_rsem.at[q],
            device_id={"sector": partner},
            device_id_type=MESH,
        )

    def far_copy(q, to):
        return pltpu.make_async_remote_copy(
            src_ref=far_send[q].at[to % half],
            dst_ref=in_recv[q].at[partner],
            send_sem=far_ssem.at[q, to % half],
            recv_sem=in_rsem.at[q, partner],
            device_id={"sector": to},
            device_id_type=MESH,
        )

    def direct(p):
        return inner | (p // half == mine)

    def nearby(o):
        return mine * half + lax.rem(me % half + o, half)

    pl.semaphore_wait(barrier, n - 1)

    for q in range(CHUNKS):

        @pl.when(jnp.logical_not(inner))
        def _():
            raw_copy(q).start()

        @pl.loop(0, n - 1)
        def _(t):
            p = peer(t)

            @pl.when(direct(p))
            def _():
                in_copy(q, p, me).start()

    @pl.loop(0, n)
    def _(p):
        for k, slot in enumerate(pick(p, partner)):
            take_far[p * CAP + k] = slot

    def hand_on(q):
        @pl.when(inner)
        def _():
            raw_copy(q).wait_recv()

            @pl.loop(1, half)
            def _(o):
                p = nearby(o)
                for k in range(CAP):
                    far_send[q][p % half, k] = raw[q][take_far[p * CAP + k]]
                far_copy(q, p).start()

            for k in range(CAP):
                in_recv[q][partner, k] = raw[q][take_far[me * CAP + k]]

    tile = 16
    for b in range(envs):
        load_right(b).wait()

    @pl.loop(0, envs * width // tile)
    def _(i):
        b = i // (width // tile)
        r = (i % (width // tile)) * tile
        r = pl.multiple_of(r, tile)
        block = jnp.swapaxes(raw_r[b, pl.ds(r, tile)], 0, 1)
        for w in range(terms):
            flat_r[pl.ds(pl.multiple_of(b * width + r, tile), tile), w * width : (w + 1) * width] = block[w]

    hand_on(0)

    for a in range(envs):
        load_left(a).wait()

    @pl.loop(0, envs * width // tile)
    def _(i):
        a = i // (width // tile)
        x = (i % (width // tile)) * tile
        x = pl.multiple_of(x, tile)
        q = x // part
        block = jnp.swapaxes(raw_l[a, pl.ds(x, tile)], 0, 1)
        at = pl.multiple_of(q * envs * part + a * part + x % part, tile)
        for w in range(terms):
            flat_l[pl.ds(at, tile), w * width : (w + 1) * width] = block[w]

    @pl.loop(0, n)
    def _(j):
        hits = two_hits(town, j * rows, rows, me, lambda row: tslot[j * rows + row], -1)
        for k in range(CAP):
            landing[j * CAP + k] = hits[k]

    @pl.loop(0, half)
    def _(h):
        base = (mine * half + h) * rows
        hits = two_hits(town, base, rows, partner, lambda row: tslot[base + row], -1)
        for k in range(CAP):
            landing_far[h * CAP + k] = hits[k]

    hand_on(1)
    acc[...] = jnp.zeros_like(acc)
    load_dav.wait()

    @pl.loop(0, rows)
    def _(i):
        owner = sown[me * rows + i]

        def count(h, seen):
            same = (sown[me * rows + h] == owner) & (h < i)
            return seen + same.astype(jnp.int32)

        rank = lax.fori_loop(0, rows, count, jnp.int32(0), unroll=16)
        rank_of[i] = owner * CAP + jnp.minimum(rank, CAP - 1)

    @pl.loop(0, n)
    def _(p):
        hits = two_hits(town, me * rows, rows, p, lambda row: row, 0)
        for k in range(CAP):
            chosen[p * CAP + k] = hits[k]

    for q in range(CHUNKS):

        @pl.loop(0, n - 1)
        def _(t):
            owner = source(t)

            @pl.when(jnp.logical_not(inner & (owner == partner)))
            def _():
                in_copy(q, owner, owner).wait_recv()

        @pl.loop(0, rows)
        def _(i):
            at = rank_of[i]
            b = i // repeats
            c = i % repeats
            operand[
                pl.ds(pl.multiple_of(c * part, part), part),
                pl.ds(pl.multiple_of(b * width, width), width),
            ] = in_recv[q][at // CAP, at % CAP]

        @pl.loop(0, terms // 2)
        def _(pair):
            cols = pl.ds(pl.multiple_of(pair * 2 * width, 2 * width), 2 * width)
            out = jnp.dot(
                operand[...], flat_r[:, cols], preferred_element_type=jnp.float32
            ).astype(jnp.bfloat16)
            for c in range(repeats):
                for h in range(2):
                    at = pl.multiple_of((pair * 2 + h) * width + q * part, part)
                    contracted[pl.ds(at, part), c * width : (c + 1) * width] = out[
                        c * part : (c + 1) * part, h * width : (h + 1) * width
                    ]

    def out_copy(q, to, frm):
        return pltpu.make_async_remote_copy(
            src_ref=out_send[q].at[to],
            dst_ref=out_recv[q].at[frm],
            send_sem=out_ssem.at[q, to],
            recv_sem=out_rsem.at[q, frm],
            device_id={"sector": to},
            device_id_type=MESH,
        )

    def gather_copy(q, p, to, frm):
        return pltpu.make_async_remote_copy(
            src_ref=out_send[q].at[p],
            dst_ref=gath[q].at[frm],
            send_sem=out_ssem.at[q, p],
            recv_sem=gath_rsem.at[q, frm],
            device_id={"sector": to},
            device_id_type=MESH,
        )

    def sum_copy(q):
        return pltpu.make_async_remote_copy(
            src_ref=sum_send[q],
            dst_ref=sum_recv[q],
            send_sem=sum_ssem.at[q],
            recv_sem=sum_rsem.at[q],
            device_id={"sector": partner},
            device_id_type=MESH,
        )

    quarter = half // 2
    far_end = jnp.where(mine == 0, 3, 0) * quarter

    def reached(p):
        return (p // half == mine) | ((p // quarter) % 3 != 0)

    for q in range(CHUNKS):
        lhs_rows = slice(q * envs * part, (q + 1) * envs * part)

        @pl.loop(0, repeats // 2)
        def _(pair):
            cols = pl.ds(pl.multiple_of(pair * 2 * width, 2 * width), 2 * width)
            out = jnp.dot(
                flat_l[lhs_rows, :], contracted[:, cols], preferred_element_type=jnp.float32
            ).astype(jnp.bfloat16)
            for a in range(envs):
                for h in range(2):
                    res[q][a * repeats + pair * 2 + h] = out[
                        a * part : (a + 1) * part, h * width : (h + 1) * width
                    ]

        @pl.loop(0, quarter)
        def _(i):
            p = far_end + i
            to = lax.rem(p + half, n)
            for k in range(CAP):
                out_send[q][p, k] = res[q][chosen[p * CAP + k]]

            @pl.when(to != me)
            def _():
                gather_copy(q, p, to, me % half).start()

        @pl.when(inner)
        def _():
            for k in range(CAP):
                gath[q][me % half, k] = res[q][chosen[partner * CAP + k]]

        @pl.loop(0, n - 1)
        def _(t):
            p = peer(t)

            @pl.when(reached(p))
            def _():
                for k in range(CAP):
                    out_send[q][p, k] = res[q][chosen[p * CAP + k]]
                out_copy(q, p, me).start()

        for k in range(CAP):
            out_recv[q][me, k] = res[q][chosen[me * CAP + k]]

    tile = 16
    for q in range(CHUNKS):

        @pl.when(inner)
        def _():
            @pl.loop(1, half)
            def _(o):
                frm = lax.rem(me % half + o, half)
                gather_copy(q, partner, me, frm).wait_recv()

            @pl.loop(0, part // tile)
            def _(i):
                at = pl.ds(pl.multiple_of(i * tile, tile), tile)

                def gather(frm, totals):
                    totals = list(totals)
                    for k in range(CAP):
                        value = gath[q][frm, k, at].astype(jnp.float32)
                        land = landing_far[frm * CAP + k]
                        for b in range(owned):
                            totals[b] = totals[b] + jnp.where(land == b, 1.0, 0.0) * value
                    return tuple(totals)

                zero = tuple(jnp.zeros((tile, width), jnp.float32) for _ in range(owned))
                totals = lax.fori_loop(0, half, gather, zero, unroll=4)
                for b in range(owned):
                    sum_send[q][b, at] = totals[b].astype(jnp.bfloat16)

            sum_copy(q).start()

    def add(q, j):
        values = [out_recv[q][j, k].astype(jnp.float32) for k in range(CAP)]
        lands = [landing[j * CAP + k] for k in range(CAP)]
        for d in range(owned):
            total = acc[q, d]
            for k in range(CAP):
                total = total + jnp.where(lands[k] == d, 1.0, 0.0) * values[k]
            acc[q, d] = total

    partial = [jnp.zeros((8, width), jnp.float32) for _ in range(nv)]
    for q in range(CHUNKS):
        add(q, me)

        @pl.loop(0, n - 1)
        def _(t):
            j = source(t)

            @pl.when(direct(j))
            def _():
                out_copy(q, j, j).wait_recv()
                add(q, j)

        @pl.when(jnp.logical_not(inner))
        def _():
            sum_copy(q).wait_recv()

            @pl.loop(0, owned)
            def _(d):
                acc[q, d] = acc[q, d] + sum_recv[q][d].astype(jnp.float32)

        for d in range(owned):
            block = acc[q, d].astype(jnp.bfloat16)
            applied_ref[d, q * part : (q + 1) * part, :] = block
            block = block.astype(jnp.float32)
            for v in range(nv):
                prod = dav[v, d, q * part : (q + 1) * part, :].astype(jnp.float32) * block
                partial[v] = partial[v] + jnp.sum(prod.reshape(part // 8, 8, width), axis=0)

    for v in range(nv):
        corr_send[v : v + 1, :] = jnp.sum(partial[v], axis=0, keepdims=True)
    if nv < corr_send.shape[0]:
        corr_send[nv:, :] = jnp.zeros((corr_send.shape[0] - nv, width), jnp.float32)

    def corr_copy(to, frm):
        return pltpu.make_async_remote_copy(
            src_ref=corr_send,
            dst_ref=corr_recv.at[frm],
            send_sem=corr_ssem.at[to],
            recv_sem=corr_rsem.at[frm],
            device_id={"sector": to},
            device_id_type=MESH,
        )

    @pl.loop(0, n - 1)
    def _(t):
        corr_copy(peer(t), me).start()

    store = pltpu.make_async_copy(applied_ref, applied_hbm, store_sem)
    store.start()

    corr_recv[me] = corr_send[...]

    @pl.loop(0, n - 1)
    def _(t):
        p = peer(t)
        for q in range(CHUNKS):

            @pl.when(reached(p) | (lax.rem(p + half, n) != me))
            def _():
                out_copy(q, p, me).wait_send()

            @pl.when(direct(p))
            def _():
                in_copy(q, p, me).wait_send()

    for q in range(CHUNKS):

        @pl.when(jnp.logical_not(inner))
        def _():
            raw_copy(q).wait_send()

        @pl.when(inner)
        def _():
            sum_copy(q).wait_send()

        @pl.when(inner)
        def _():
            @pl.loop(1, half)
            def _(o):
                far_copy(q, nearby(o)).wait_send()

    @pl.loop(0, n - 1)
    def _(t):
        corr_copy(source(t), source(t)).wait_recv()

    store.wait()
    total = jnp.sum(corr_recv[...], axis=0)
    for v in range(nv):
        corr_ref[v] = jnp.sum(total[v : v + 1, :])

    @pl.loop(0, n - 1)
    def _(t):
        corr_copy(peer(t), me).wait_send()


def shards(
    wave_blocks,
    davidson_basis,
    left_env,
    right_env,
    source_owner,
    source_slot,
    target_owner,
    target_slot,
):
    n = lax.axis_size("sector")
    owned, width = wave_blocks.shape[0], wave_blocks.shape[1]
    envs, terms = right_env.shape[0], right_env.shape[2]
    rows = source_slot.shape[0] // n
    repeats = rows // envs
    nv = davidson_basis.shape[0]
    part = width // CHUNKS
    corr_rows = -(-nv // 8) * 8
    bf16 = jnp.bfloat16
    smem = pl.BlockSpec(memory_space=pltpu.SMEM)
    hbm = pl.BlockSpec(memory_space=pl.ANY)
    dma = pltpu.SemaphoreType.DMA
    flops = 4 * rows * terms * width**3
    return pl.pallas_call(
        functools.partial(kernel, n, repeats),
        out_shape=(
            jax.ShapeDtypeStruct((owned, width, width), bf16),
            jax.ShapeDtypeStruct((nv,), jnp.float32),
        ),
        in_specs=[hbm] * 8,
        out_specs=(hbm, smem),
        scratch_shapes=[
            pltpu.SMEM((rows * n,), jnp.int32),
            pltpu.SMEM((rows * n,), jnp.int32),
            pltpu.SMEM((rows * n,), jnp.int32),
            pltpu.SMEM((rows * n,), jnp.int32),
            pltpu.VMEM((owned, width, width), bf16),
            dma((4,)),
            dma,
            pltpu.VMEM((owned, width, width), bf16),
            pltpu.VMEM((nv, owned, width, width), bf16),
            pltpu.VMEM((envs, width, terms, width), bf16),
            pltpu.VMEM((envs, width, terms, width), bf16),
            pltpu.VMEM((envs * width, terms * width), bf16),
            pltpu.VMEM((envs * width, terms * width), bf16),
            pltpu.VMEM((n, CAP, part, width), bf16),
            pltpu.VMEM((n, CAP, part, width), bf16),
            pltpu.VMEM((n, CAP, part, width), bf16),
            pltpu.VMEM((n, CAP, part, width), bf16),
            pltpu.VMEM((repeats * part, envs * width), bf16),
            pltpu.VMEM((terms * width, repeats * width), bf16),
            pltpu.VMEM((rows, part, width), bf16),
            pltpu.VMEM((rows, part, width), bf16),
            pltpu.VMEM((n, CAP, part, width), bf16),
            pltpu.VMEM((n, CAP, part, width), bf16),
            pltpu.VMEM((n, CAP, part, width), bf16),
            pltpu.VMEM((n, CAP, part, width), bf16),
            pltpu.VMEM((CHUNKS, owned, part, width), jnp.float32),
            pltpu.VMEM((nv, 8, width), jnp.float32),
            pltpu.VMEM((corr_rows, width), jnp.float32),
            pltpu.VMEM((n, corr_rows, width), jnp.float32),
            pltpu.SMEM((n * CAP,), jnp.int32),
            pltpu.SMEM((n * CAP,), jnp.int32),
            pltpu.SMEM((n * CAP,), jnp.int32),
            pltpu.SMEM((rows,), jnp.int32),
            pltpu.SMEM((n * CAP,), jnp.int32),
            pltpu.VMEM((owned, part, width), bf16),
            pltpu.VMEM((owned, part, width), bf16),
            pltpu.VMEM((n // 2, CAP, part, width), bf16),
            pltpu.VMEM((n // 2, CAP, part, width), bf16),
            dma((CHUNKS,)),
            dma((CHUNKS,)),
            dma((CHUNKS, n // 2)),
            pltpu.VMEM((n // 2, CAP, part, width), bf16),
            pltpu.VMEM((n // 2, CAP, part, width), bf16),
            pltpu.VMEM((owned, part, width), bf16),
            pltpu.VMEM((owned, part, width), bf16),
            pltpu.VMEM((owned, part, width), bf16),
            pltpu.VMEM((owned, part, width), bf16),
            pltpu.SMEM((n // 2 * CAP,), jnp.int32),
            dma((CHUNKS, n // 2)),
            dma((CHUNKS,)),
            dma((CHUNKS,)),
            dma((2,)),
            dma((envs,)),
            dma((envs,)),
            dma((CHUNKS, n)),
            dma((CHUNKS, n)),
            dma((CHUNKS, n)),
            dma((CHUNKS, n)),
            dma((n,)),
            dma((n,)),
        ],
        compiler_params=pltpu.CompilerParams(
            collective_id=0, has_side_effects=True, vmem_limit_bytes=60 * 2**20
        ),
        cost_estimate=pl.CostEstimate(
            flops=flops, bytes_accessed=10 * 2**20, transcendentals=0
        ),
    )(
        source_owner.reshape(-1),
        source_slot,
        target_owner.reshape(-1),
        target_slot,
        wave_blocks,
        davidson_basis,
        left_env,
        right_env,
    )


def solution(mesh):
    return jax.shard_map(
        shards,
        mesh=mesh,
        in_specs=(
            P(("groups", "sector"), None, None),
            P(None, ("groups", "sector"), None, None),
            P(("groups", "sector"), None, None, None),
            P(("groups", "sector"), None, None, None),
            P("groups", None),
            P("groups"),
            P("groups", None),
            P("groups"),
        ),
        out_specs=(P(("groups", "sector"), None, None), P("groups")),
        check_vma=False,
    )
```
